32 devices in a mesh: seq: 8 (over y, x, core), head: 4 (over z).
Axes of the slice: x: 2, y: 2, z: 4, core: 2. Of those that a mesh axis runs over, the one named last changes fastest.
Arguments:
- x_in: bfloat16 [2048, 8192], P('seq', 'head'), may hold values from -6 to 6
- b_in: bfloat16 [2048, 128], P(('seq', 'head')), may hold values from -0.625 to 0.625
- c_in: bfloat16 [2048, 128], P(('seq', 'head')), may hold values from -0.625 to 0.625
- decay_codes: int32 [128, 2048], P('head', 'seq'), may hold values from 0 to 7168
- decay_rate: float32 [128], P('head'), may hold values from 0 to 0.05
- skip_gain: float32 [128], P('head'), may hold values from 0.5 to 1.5
- out_grad: bfloat16 [2048, 8192], P('seq', 'head'), may hold values from -6 to 6
Outputs:
- ssm_out: bfloat16 [2048, 8192], P('seq', 'head')
- input_grad: bfloat16 [2048, 8192], P('seq', 'head')
- grad_b: float32 [2048, 128], P(('seq', 'head'))
- grad_c: float32 [2048, 128], P(('seq', 'head'))
The draws below stay inside these ranges and needn't reach their ends.
All inputs are finite; a program needn't handle non-finite values.
Results may differ from the reference program's by a relative error of at most 0.005.
Values may be sent and summed in bfloat16 or wider, within the bound.
A program may use at most 64 MiB of HBM per device.

```python
import jax
import jax.numpy as jnp
from jax import lax

HEADS = 128
HEAD_DIM = 64
STATE = 128
BLOCK = 256
TOKENS = 2048


def draw_decay_codes(key, part):
    base_key, place_key, level_key = jax.random.split(jax.random.fold_in(key, 17), 3)
    base = jax.random.randint(base_key, (HEADS, TOKENS), 0, 1024)
    places = jax.random.permutation(place_key, TOKENS)[:3]
    levels = jax.random.randint(level_key, (HEADS, 3), 2, 7)
    matches = (jnp.arange(TOKENS)[:, None] == places[None, :]).astype(jnp.int32)
    raised = jnp.einsum('hs,ts->ht', levels, matches)
    return (base + 1024 * raised).astype(jnp.int32)


def draw_decay_rate(key, part):
    pick_key, value_key = jax.random.split(jax.random.fold_in(key, 23))
    slow_share = 0.7
    picks = jax.random.uniform(pick_key, (HEADS,))
    spread = jax.random.uniform(value_key, (HEADS,))
    slow_rate = jnp.exp(jnp.log(0.2 / TOKENS) + spread * jnp.log(5.0))
    fast_rate = jnp.exp(jnp.log(0.02) + spread * jnp.log(50.0 / 30.0))
    return jnp.where(picks < slow_share, slow_rate, fast_rate).astype(jnp.float32)


def block_scale(own_key, shape, cuts, least, largest):
    level = 1.0
    for dim, shards_of in cuts:
        heights = jax.random.uniform(jax.random.fold_in(jax.random.fold_in(own_key, 6), dim), (shards_of,), jnp.float32, least / len(cuts), largest / len(cuts))
        level = level * jnp.repeat(jnp.exp(heights), shape[dim] // shards_of).reshape((-1,) + (1,) * (len(shape) - 1 - dim))
    return level


def normal_values(key, extent, deviation, limit, cuts=(), kind=jnp.bfloat16):
    array = jax.random.normal(key, extent, jnp.float32) * deviation
    if len(cuts) > 0:
        array = block_scale(key, extent, cuts, -0.22, 0.18) * array
    return jnp.clip(array, min=-limit, max=limit).astype(kind)


def setup_inputs(seed: int = 0) -> dict:
    key_of = jax.random.split(jax.random.key(seed), 8)
    return {
        "x_in": normal_values(key_of[0], (TOKENS, HEADS * HEAD_DIM), 1.0, 6.0, ((0, 8), (1, 4))),
        "b_in": normal_values(key_of[1], (TOKENS, STATE), ((STATE * TOKENS) ** -0.25), 0.625, ((0, 32),)),
        "c_in": normal_values(key_of[2], (TOKENS, STATE), ((STATE * TOKENS) ** -0.25), 0.625, ((0, 32),)),
        "decay_codes": draw_decay_codes(jax.random.fold_in(key_of[7], 71), 0),
        "decay_rate": draw_decay_rate(jax.random.fold_in(key_of[7], 71), 0),
        "skip_gain": jnp.clip(0.5 + 1.0 * jax.random.uniform(key_of[5], (HEADS,), jnp.float32) ** block_scale(key_of[5], (HEADS,), ((0, 4),), -0.2, 0.2), 0.5, 1.5),
        "out_grad": normal_values(key_of[6], (TOKENS, HEADS * HEAD_DIM), 1.0, 6.0, ((0, 8), (1, 4))),
    }


def exact(form, operands):
    return jnp.einsum(form, *operands, precision=lax.Precision.HIGHEST)


def decode(decay_labels, decay_speeds):
    time_delta = 0.5 + (decay_labels % 1024).astype(jnp.float32) / 1024.0
    spike_loss_term = 0.1 * (decay_labels // 1024).astype(jnp.float32)
    return time_delta, -decay_speeds[:, None] * time_delta - spike_loss_term


def summarize(cumul, b_block, c_block, driven, cotangent):
    tail = jnp.exp(cumul[:, -1:] - cumul)
    state_part = exact("hj,jn,jhp->hpn", (tail, b_block.astype(jnp.float32), driven))
    adjoint_part = exact("hi,in,ihp->hpn", (jnp.exp(cumul), c_block.astype(jnp.float32), cotangent))
    return state_part, adjoint_part


def within(cumul, b_block, c_block, driven, cotangent):
    width = cumul.shape[1]
    causal = lax.broadcasted_iota(jnp.int32, (width, width), 0) >= lax.broadcasted_iota(jnp.int32, (width, width), 1)
    spread = cumul[:, :, None] - cumul[:, None, :]
    weights = jnp.where(causal, jnp.exp(jnp.where(causal, spread, 0.0)), 0.0)
    scores = jnp.dot(c_block, b_block.T, preferred_element_type=jnp.float32)
    mixed = (weights * scores).astype(jnp.bfloat16).astype(jnp.float32)
    out_part = exact("hij,jhp->ihp", (mixed, driven))
    drive_grad = exact("hij,ihp->jhp", (mixed, cotangent))
    paired = (weights * exact("ihp,jhp->hij", (cotangent, driven))).astype(jnp.bfloat16).astype(jnp.float32)
    c_grad = exact("hij,jn->in", (paired, b_block.astype(jnp.float32)))
    b_grad = exact("hij,in->jn", (paired, c_block.astype(jnp.float32)))
    return out_part, drive_grad, c_grad, b_grad


def reference(x_in, b_in, c_in, decay_codes, decay_rate, skip_gain, out_grad):
    head_count, token_count = decay_codes.shape
    blocks = token_count // BLOCK
    time_delta, log_decay = decode(decay_codes, decay_rate)
    inputs = x_in.astype(jnp.float32).reshape(blocks, BLOCK, head_count, HEAD_DIM)
    cotangent = out_grad.astype(jnp.float32).reshape(blocks, BLOCK, head_count, HEAD_DIM)
    step_tokens = time_delta.reshape(head_count, blocks, BLOCK).transpose(1, 2, 0)[..., None]
    driven = (inputs * step_tokens).astype(jnp.bfloat16).astype(jnp.float32)
    cumul = jnp.cumsum(log_decay.reshape(head_count, blocks, BLOCK), axis=2).transpose(1, 0, 2)
    input_matrix_blocks = b_in.reshape(blocks, BLOCK, STATE)
    c_blocks = c_in.reshape(blocks, BLOCK, STATE)
    blank_state = jnp.zeros((head_count, HEAD_DIM, STATE), jnp.float32)

    def ahead(running, group):
        cumul_b, b_block, c_block, driven_b, cot_b = group
        state_part, adjoint_part = summarize(cumul_b, b_block, c_block, driven_b, cot_b)
        out_part, drive_grad, c_grad, b_grad = within(cumul_b, b_block, c_block, driven_b, cot_b)
        growth = jnp.exp(cumul_b)
        out_cross = exact("hi,hpn,in->ihp", (growth, running, c_block.astype(jnp.float32)))
        c_cross = exact("hi,ihp,hpn->in", (growth, cot_b, running))
        next_device_state = jnp.exp(cumul_b[:, -1])[:, None, None] * running + state_part
        return next_device_state, (out_part + out_cross, c_grad + c_cross, drive_grad, b_grad, adjoint_part)

    last_state, gathered = lax.scan(ahead, blank_state, (cumul, input_matrix_blocks, c_blocks, driven, cotangent))
    out_sum, c_sum, drive_grad, b_grad, adjoint_parts = gathered

    def behind(running, group):
        cumul_b, b_block, driven_b, adjoint_part = group
        tail = jnp.exp(cumul_b[:, -1:] - cumul_b)
        drive_cross = exact("hj,hpn,jn->jhp", (tail, running, b_block.astype(jnp.float32)))
        b_cross = exact("hj,jhp,hpn->jn", (tail, driven_b, running))
        next_device_state = jnp.exp(cumul_b[:, -1])[:, None, None] * running + adjoint_part
        return next_device_state, (drive_cross, b_cross)

    first_adjoint, crossed = lax.scan(behind, blank_state, (cumul, input_matrix_blocks, driven, adjoint_parts), reverse=True)
    drive_cross, b_cross = crossed
    gain = skip_gain[None, None, :, None]
    ssm_out = (out_sum + gain * inputs).astype(jnp.bfloat16).reshape(token_count, head_count * HEAD_DIM)
    input_grad = (gain * cotangent + step_tokens * (drive_grad + drive_cross)).astype(jnp.bfloat16)
    input_grad = input_grad.reshape(token_count, head_count * HEAD_DIM)
    grad_b = (b_grad + b_cross).reshape(token_count, STATE)
    grad_c = c_sum.reshape(token_count, STATE)
    return ssm_out, input_grad, grad_b, grad_c
```

```python
import functools

import jax
import jax.numpy as jnp
from jax import lax
from jax.experimental import pallas as pl
from jax.experimental.pallas import tpu as pltpu
from jax.sharding import PartitionSpec as P

SUB = 128
MESH = pl.DeviceIdType.MESH
F32 = jnp.float32
BF16 = jnp.bfloat16


def dot(a, b, dims=((1,), (0,))):
    return lax.dot_general(a, b, (dims, ((), ())), preferred_element_type=F32)


def split3(a):
    hi = a.astype(BF16).astype(F32)
    mid = (a - hi).astype(BF16).astype(F32)
    low = a - hi - mid
    return jnp.concatenate([hi, mid, low], axis=0).astype(BF16)


def split_dot(a, b, dims=((1,), (0,))):
    hi = a.astype(BF16)
    low = (a - hi.astype(F32)).astype(BF16)
    return dot(hi, b, dims) + dot(low, b, dims)


def kernel(
    chips, zs,
    x_ref, b_ref, c_ref, codes_ref, rate_ref, gain_ref, g_ref,
    out_ref, ig_ref, gb_ref, gc_ref,
    u_s, vs_s, ug_s, vx_s, od_s, gd_s, ps_s, as_s, gain_s,
    bc, pa, dd, pc, dc, qb, qt, rq, rt, tmp, ef, part, rpart,
    g_send, g_recv, s_send, s_recv, q_send, q_recv, t_send, t_recv, r_send, r_recv,
):
    tokens, width = x_ref.shape
    heads = codes_ref.shape[0]
    dim = width // heads
    state = b_ref.shape[1]
    rows = b_ref.shape[0]
    subs = tokens // SUB
    half = width // 2
    seq = lax.axis_index("seq")
    z = lax.axis_index("head")
    chip = seq // 2
    core = seq % 2
    other = 1 - core
    sib = {"seq": chip * 2 + other, "head": z}

    def z_peer(d):
        return {"seq": seq, "head": (z + d) % zs}

    def chip_peer(d):
        return {"seq": ((chip + d) % chips) * 2 + core, "head": z}

    def copy(src, dst, send, recv, to):
        return pltpu.make_async_remote_copy(
            src_ref=src, dst_ref=dst, send_sem=send, recv_sem=recv,
            device_id=to, device_id_type=MESH,
        )

    barrier = pltpu.get_barrier_semaphore()
    for d in range(1, zs):
        pl.semaphore_signal(barrier, inc=1, device_id=z_peer(d), device_id_type=MESH)
    for d in range(1, chips):
        pl.semaphore_signal(barrier, inc=1, device_id=chip_peer(d), device_id_type=MESH)
    pl.semaphore_signal(barrier, inc=1, device_id=sib, device_id_type=MESH)
    bc[z, 0] = b_ref[...]
    bc[z, 1] = c_ref[...]
    pl.semaphore_wait(barrier, zs + chips - 1)

    gathers = [
        copy(bc.at[z], bc.at[z], g_send.at[d - 1], g_recv.at[d - 1], z_peer(d))
        for d in range(1, zs)
    ]
    for each in gathers:
        each.start()

    eye = lax.broadcasted_iota(jnp.int32, (heads, heads), 0) == lax.broadcasted_iota(
        jnp.int32, (heads, heads), 1
    )
    rate = jnp.sum(jnp.where(eye, rate_ref[...], 0.0), axis=1, keepdims=True)
    gain = jnp.sum(jnp.where(eye, gain_ref[...], 0.0), axis=1, keepdims=True)
    codes = codes_ref[...]
    step = 0.5 + (codes & 1023).astype(F32) * (1.0 / 1024.0)
    log_decay = -rate * step - 0.1 * (codes >> 10).astype(F32)
    at_u = lax.broadcasted_iota(jnp.int32, (tokens, tokens), 0)
    at_t = lax.broadcasted_iota(jnp.int32, (tokens, tokens), 1)
    centred = jnp.where(
        at_u // SUB == at_t // SUB, jnp.where(at_u <= at_t, 0.5, -0.5), 0.0
    ).astype(BF16)
    logs = dot(split3(log_decay), centred)
    logs = logs[:heads] + logs[heads : 2 * heads] + logs[2 * heads :]
    u3 = split3(jnp.exp(logs))
    v3 = split3(jnp.exp(-logs) * step)
    head_of = lax.broadcasted_iota(jnp.int32, (heads, width), 1) // dim
    spread = (head_of == lax.broadcasted_iota(jnp.int32, (heads, width), 0)).astype(F32)
    gain_s[...] = jnp.sum(spread * gain, axis=0, keepdims=True)
    spread3 = jnp.concatenate([spread] * 3, axis=0).astype(BF16)
    u_s[...] = dot(u3, spread3, ((0,), (0,)))
    vs_s[...] = dot(v3, spread3, ((0,), (0,)))
    ug_s[...] = (u_s[...] * g_ref[...].astype(F32)).astype(BF16)
    vx_s[...] = (vs_s[...] * x_ref[...].astype(F32)).astype(BF16)

    for each in gathers:
        each.wait()
    b_all = bc[:, 0].reshape(tokens, state)
    c_all = bc[:, 1].reshape(tokens, state)

    def block(a):
        return slice(a * SUB, (a + 1) * SUB)

    def root(a, lanes):
        return u_s[(a + 1) * SUB - 1 : (a + 1) * SUB, lanes]

    halves = [slice(0, half), slice(half, width)]
    for h, lanes in enumerate(halves):
        total = None
        for a in range(subs):
            r = root(a, lanes)
            ps = r * dot(b_all[block(a)], vx_s[block(a), lanes], ((0,), (0,)))
            ad = r * dot(c_all[block(a)], ug_s[block(a), lanes], ((0,), (0,)))
            ps_s[a, :, lanes] = ps
            as_s[a, :, lanes] = ad
            if a == 0:
                p_dev, a_dev, total = ps, ad, r * r
            else:
                p_dev = (r * r) * p_dev + ps
                a_dev = a_dev + total * ad
                total = total * (r * r)
        pa[h, 0] = p_dev.astype(BF16)
        pa[h, 1] = a_dev.astype(BF16)
        dd[h] = total

    to_sib = [
        copy(pa.at[other], pc.at[core], s_send.at[0], s_recv.at[0], sib),
        copy(dd.at[other], dc.at[core], s_send.at[1], s_recv.at[1], sib),
    ]
    for each in to_sib:
        each.start()
    pc[core] = pa[core]
    dc[core] = dd[core]
    for each in to_sib:
        each.wait()
    p0, p1 = pc[0, 0].astype(F32), pc[1, 0].astype(F32)
    a0, a1 = pc[0, 1].astype(F32), pc[1, 1].astype(F32)
    qb[0] = (dc[1] * p0 + p1).astype(BF16)
    qb[1] = (a0 + dc[0] * a1).astype(BF16)
    qt[...] = dc[0] * dc[1]
    to_chips = []
    for d in range(1, chips):
        kind = (chip + d) // chips
        to_chips.append(
            copy(qb.at[kind], rq.at[d - 1], q_send.at[d - 1], q_recv.at[d - 1], chip_peer(d))
        )
        to_chips.append(
            copy(qt, rt.at[d - 1], t_send.at[d - 1], t_recv.at[d - 1], chip_peer(d))
        )
    for each in to_chips:
        each.start()

    at_r = lax.broadcasted_iota(jnp.int32, (SUB, SUB), 0)
    at_c = lax.broadcasted_iota(jnp.int32, (SUB, SUB), 1)
    sums = []
    for a in range(subs):
        b_a, c_a = b_all[block(a)], c_all[block(a)]
        scores = jnp.where(at_r >= at_c, dot(c_a, b_a, ((1,), (1,))), 0.0).astype(BF16)
        flipped = jnp.where(at_r <= at_c, dot(b_a, c_a, ((1,), (1,))), 0.0).astype(BF16)
        od_s[block(a)] = dot(scores, vx_s[block(a)])
        gd_s[block(a)] = dot(flipped, ug_s[block(a)])
        paired = dot(ug_s[block(a)], vx_s[block(a)], ((1,), (1,)))
        paired = jnp.where(at_r >= at_c, paired, 0.0)
        sums.append((split_dot(paired.T, c_a), split_dot(paired, b_a)))

    for each in to_chips:
        each.wait()
    e_in = jnp.zeros((state, half), F32)
    f_in = jnp.zeros((state, half), F32)
    reach = jnp.ones((1, half), F32)
    for d in range(1, chips):
        e_in = e_in + jnp.where(chip >= d, reach, 0.0) * rq[d - 1].astype(F32)
        reach = reach * rt[d - 1]
    reach = jnp.ones((1, half), F32)
    for d in range(chips - 1, 0, -1):
        f_in = f_in + jnp.where(chip < d, reach, 0.0) * rq[d - 1].astype(F32)
        reach = reach * rt[d - 1]
    tmp[0, 0] = e_in.astype(BF16)
    tmp[1, 0] = (dc[0] * e_in + pc[0, 0].astype(F32)).astype(BF16)
    tmp[1, 1] = f_in.astype(BF16)
    tmp[0, 1] = (dc[1] * f_in + pc[1, 1].astype(F32)).astype(BF16)
    back = copy(tmp.at[other], ef.at[core], s_send.at[2], s_recv.at[2], sib)
    back.start()
    ef[core] = tmp[core]
    back.wait()

    states = {}
    for h, lanes in enumerate(halves):
        e = ef[h, 0].astype(F32)
        f = ef[h, 1].astype(F32)
        for a in range(subs):
            r = root(a, lanes)
            states[h, a, 0] = (r * e).astype(BF16)
            e = (r * r) * e + ps_s[a, :, lanes]
        for a in range(subs - 1, -1, -1):
            r = root(a, lanes)
            states[h, a, 1] = (r * f).astype(BF16)
            f = (r * r) * f + as_s[a, :, lanes]
    b_sums, c_sums = [], []
    for a in range(subs):
        b_sum, c_sum = sums[a]
        for h, lanes in enumerate(halves):
            b_sum = b_sum + dot(vx_s[block(a), lanes], states[h, a, 1], ((1,), (1,)))
            c_sum = c_sum + dot(ug_s[block(a), lanes], states[h, a, 0], ((1,), (1,)))
        b_sums.append(b_sum)
        c_sums.append(c_sum)
    part[:, 0] = jnp.concatenate(b_sums, axis=0).reshape(zs, rows, state)
    part[:, 1] = jnp.concatenate(c_sums, axis=0).reshape(zs, rows, state)
    scatters = [
        copy(part.at[(z + d) % zs], rpart.at[d - 1], r_send.at[d - 1], r_recv.at[d - 1], z_peer(d))
        for d in range(1, zs)
    ]
    for each in scatters:
        each.start()
    for a in range(subs):
        for h, lanes in enumerate(halves):
            out = od_s[block(a), lanes] + dot(c_all[block(a)], states[h, a, 0])
            out = u_s[block(a), lanes] * out
            out = out + gain_s[:, lanes] * x_ref[block(a), lanes].astype(F32)
            out_ref[block(a), lanes] = out.astype(BF16)
            grad = gd_s[block(a), lanes] + dot(b_all[block(a)], states[h, a, 1])
            grad = vs_s[block(a), lanes] * grad
            grad = grad + gain_s[:, lanes] * g_ref[block(a), lanes].astype(F32)
            ig_ref[block(a), lanes] = grad.astype(BF16)
    gb, gc = part[z, 0], part[z, 1]
    for d, each in enumerate(scatters):
        each.wait()
        gb = gb + rpart[d, 0]
        gc = gc + rpart[d, 1]
    gb_ref[...] = gb
    gc_ref[...] = gc


def local(x_in, b_in, c_in, decay_codes, decay_rate, skip_gain, out_grad):
    tokens, width = x_in.shape
    rows, state = b_in.shape
    heads = decay_codes.shape[0]
    subs = tokens // SUB
    half = width // 2
    chips = lax.axis_size("seq") // 2
    zs = lax.axis_size("head")
    vmem = pl.BlockSpec(memory_space=pltpu.VMEM)
    dma = pltpu.SemaphoreType.DMA
    return pl.pallas_call(
        functools.partial(kernel, chips, zs),
        out_shape=(
            jax.ShapeDtypeStruct((tokens, width), BF16),
            jax.ShapeDtypeStruct((tokens, width), BF16),
            jax.ShapeDtypeStruct((rows, state), F32),
            jax.ShapeDtypeStruct((rows, state), F32),
        ),
        in_specs=[vmem] * 7,
        out_specs=(vmem,) * 4,
        scratch_shapes=[
            pltpu.VMEM((tokens, width), F32),
            pltpu.VMEM((tokens, width), F32),
            pltpu.VMEM((tokens, width), BF16),
            pltpu.VMEM((tokens, width), BF16),
            pltpu.VMEM((tokens, width), F32),
            pltpu.VMEM((tokens, width), F32),
            pltpu.VMEM((subs, state, width), F32),
            pltpu.VMEM((subs, state, width), F32),
            pltpu.VMEM((1, width), F32),
            pltpu.VMEM((zs, 2, rows, state), BF16),
            pltpu.VMEM((2, 2, state, half), BF16),
            pltpu.VMEM((2, 1, half), F32),
            pltpu.VMEM((2, 2, state, half), BF16),
            pltpu.VMEM((2, 1, half), F32),
            pltpu.VMEM((2, state, half), BF16),
            pltpu.VMEM((1, half), F32),
            pltpu.VMEM((chips - 1, state, half), BF16),
            pltpu.VMEM((chips - 1, 1, half), F32),
            pltpu.VMEM((2, 2, state, half), BF16),
            pltpu.VMEM((2, 2, state, half), BF16),
            pltpu.VMEM((zs, 2, rows, state), F32),
            pltpu.VMEM((zs - 1, 2, rows, state), F32),
            dma((zs - 1,)), dma((zs - 1,)),
            dma((3,)), dma((3,)),
            dma((chips - 1,)), dma((chips - 1,)),
            dma((chips - 1,)), dma((chips - 1,)),
            dma((zs - 1,)), dma((zs - 1,)),
        ],
        compiler_params=pltpu.CompilerParams(
            collective_id=0, has_side_effects=True, vmem_limit_bytes=48 * 1024 * 1024
        ),
    )(
        x_in, b_in, c_in, decay_codes,
        decay_rate.reshape(1, heads), skip_gain.reshape(1, heads), out_grad,
    )


def solution(mesh):
    placed = (
        P("seq", "head"),
        P(("seq", "head"), None),
        P(("seq", "head"), None),
        P("head", "seq"),
        P("head"),
        P("head"),
        P("seq", "head"),
    )
    return jax.shard_map(
        local,
        mesh=mesh,
        in_specs=placed,
        out_specs=(
            P("seq", "head"),
            P("seq", "head"),
            P(("seq", "head"), None),
            P(("seq", "head"), None),
        ),
        check_vma=False,
    )
```

```python
import functools

import jax
import jax.numpy as jnp
from jax import lax
from jax.experimental import pallas as pl
from jax.experimental.pallas import tpu as pltpu
from jax.sharding import PartitionSpec as P

SUB = 128
MESH = pl.DeviceIdType.MESH
F32 = jnp.float32
BF16 = jnp.bfloat16


def dot(a, b, dims=((1,), (0,))):
    return lax.dot_general(a, b, (dims, ((), ())), preferred_element_type=F32)


def split3(a):
    hi = a.astype(BF16).astype(F32)
    mid = (a - hi).astype(BF16).astype(F32)
    low = a - hi - mid
    return jnp.concatenate([hi, mid, low], axis=0)


def split_dot(a, b, dims=((1,), (0,))):
    hi = a.astype(BF16)
    low = (a - hi.astype(F32)).astype(BF16)
    return dot(hi, b, dims) + dot(low, b, dims)


def kernel(
    chips, zs, parts,
    x_hbm, b_hbm, c_hbm, codes_hbm, rate_hbm, gain_hbm, g_hbm,
    out_hbm, ig_hbm, gb_ref, gc_ref,
    out_ref, ig_ref, x_ref, g_ref, codes_ref, rate_ref, gain_ref,
    u_s, vs_s, ug_s, vx_s, od_s, gd_s, ps_s, as_s, gain_s, spread_s,
    bc, pa, dd, pc, dc, qb, qt, rq, rt, tmp, ef, part, rpart,
    l_sem, g_send, g_recv, d_send, d_recv, s_send, s_recv, e_send, e_recv,
    q_send, q_recv, t_send, t_recv, r_send, r_recv, o_sem,
):
    tokens, width = x_ref.shape
    heads = codes_ref.shape[0]
    dim = width // heads
    rows, state = b_hbm.shape
    subs = tokens // SUB
    half = width // 2
    size = half // parts
    seq = lax.axis_index("seq")
    z = lax.axis_index("head")
    chip = seq // 2
    core = seq % 2
    other = 1 - core
    sib = {"seq": chip * 2 + other, "head": z}

    def z_peer(d):
        return {"seq": seq, "head": (z + d) % zs}

    def chip_peer(d):
        return {"seq": ((chip + d) % chips) * 2 + core, "head": z}

    def copy(src, dst, send, recv, to):
        return pltpu.make_async_remote_copy(
            src_ref=src, dst_ref=dst, send_sem=send, recv_sem=recv,
            device_id=to, device_id_type=MESH,
        )

    loads = [
        pltpu.make_async_copy(src, dst, l_sem.at[i])
        for i, (src, dst) in enumerate([
            (codes_hbm, codes_ref), (rate_hbm, rate_ref), (gain_hbm, gain_ref),
            (b_hbm, bc.at[z, 0]), (c_hbm, bc.at[z, 1]), (g_hbm, g_ref), (x_hbm, x_ref),
        ])
    ]
    for each in loads:
        each.start()
    barrier = pltpu.get_barrier_semaphore()
    for d in range(1, zs):
        pl.semaphore_signal(barrier, inc=1, device_id=z_peer(d), device_id_type=MESH)
    for d in range(1, chips):
        pl.semaphore_signal(barrier, inc=1, device_id=chip_peer(d), device_id_type=MESH)
    pl.semaphore_signal(barrier, inc=1, device_id=sib, device_id_type=MESH)
    for each in loads[:5]:
        each.wait()
    pl.semaphore_wait(barrier, zs + chips - 1)
    gathers = [
        copy(bc.at[z], bc.at[z], g_send.at[d - 1], g_recv.at[d - 1], z_peer(d))
        for d in range(1, zs)
    ]
    for each in gathers:
        each.start()

    eye = lax.broadcasted_iota(jnp.int32, (heads, heads), 0) == lax.broadcasted_iota(
        jnp.int32, (heads, heads), 1
    )
    rate = jnp.sum(jnp.where(eye, rate_ref[...], 0.0), axis=1, keepdims=True)
    gain = jnp.sum(jnp.where(eye, gain_ref[...], 0.0), axis=1, keepdims=True)
    codes = codes_ref[...]
    step = 0.5 + (codes & 1023).astype(F32) * (1.0 / 1024.0)
    log_decay = -rate * step - 0.1 * (codes >> 10).astype(F32)
    at_u = lax.broadcasted_iota(jnp.int32, (tokens, tokens), 0)
    at_t = lax.broadcasted_iota(jnp.int32, (tokens, tokens), 1)
    centred = jnp.where(
        at_u // SUB == at_t // SUB, jnp.where(at_u <= at_t, 0.5, -0.5), 0.0
    ).astype(BF16)
    logs = dot(split3(log_decay).astype(BF16), centred)
    logs = logs[:heads] + logs[heads : 2 * heads] + logs[2 * heads :]
    u3 = split3(jnp.exp(logs)).T.astype(BF16)
    v3 = split3(jnp.exp(-logs) * step).T.astype(BF16)
    lane = lax.broadcasted_iota(jnp.int32, (heads, width), 1)
    first = lax.broadcasted_iota(jnp.int32, (heads, width), 0) * dim
    own = (lane >= first) & (lane < first + dim)
    gain_s[...] = jnp.sum(jnp.where(own, gain, 0.0), axis=0, keepdims=True)
    total = jnp.exp(jnp.sum(log_decay, axis=1, keepdims=True))
    total = jnp.sum(jnp.where(own, total, 0.0), axis=0, keepdims=True)
    dd[0] = total[:, :half]
    dd[1] = total[:, half:]
    spread_s[...] = jnp.concatenate([own.astype(F32)] * 3, axis=0).astype(BF16)
    to_sib = copy(dd.at[other], dc.at[core], d_send.at[0], d_recv.at[0], sib)
    to_sib.start()
    dc[core] = dd[core]
    for each in loads[5:]:
        each.wait()

    def block(a):
        return slice(a * SUB, (a + 1) * SUB)

    def chunk(h, k):
        return slice(h * half + k * size, h * half + (k + 1) * size)

    def root(a, lanes):
        return u_s[(a + 1) * SUB - 1 : (a + 1) * SUB, lanes]

    def factors(k):
        for h in range(2):
            lanes = chunk(h, k)
            u = dot(u3, spread_s[:, lanes])
            vs = dot(v3, spread_s[:, lanes])
            u_s[:, lanes] = u
            vs_s[:, lanes] = vs
            ug_s[:, lanes] = (u * g_ref[:, lanes].astype(F32)).astype(BF16)
            vx_s[:, lanes] = (vs * x_ref[:, lanes].astype(F32)).astype(BF16)

    early = (parts + 1) // 2
    for k in range(early):
        factors(k)
    for each in gathers:
        each.wait()
    b_all = bc[:, 0].reshape(tokens, state)
    c_all = bc[:, 1].reshape(tokens, state)
    b_flip = b_all.astype(F32).T.astype(BF16)
    c_flip = c_all.astype(F32).T.astype(BF16)

    sib_copies = [
        copy(pa.at[other, k], pc.at[core, k], s_send.at[k], s_recv.at[k], sib)
        for k in range(parts)
    ]

    def summarize(k):
        for h in range(2):
            lanes = chunk(h, k)
            total = None
            for a in range(subs):
                r = root(a, lanes)
                ps = r * dot(b_flip[:, block(a)], vx_s[block(a), lanes])
                ad = r * dot(c_flip[:, block(a)], ug_s[block(a), lanes])
                ps_s[a, :, lanes] = ps
                as_s[a, :, lanes] = ad
                if a == 0:
                    p_dev, a_dev, total = ps, ad, r * r
                else:
                    p_dev = (r * r) * p_dev + ps
                    a_dev = a_dev + total * ad
                    total = total * (r * r)
            pa[h, k, 0] = p_dev
            pa[h, k, 1] = a_dev
        sib_copies[k].start()
        pc[core, k] = pa[core, k]

    to_chips = {}

    def combine(k):
        here = slice(k * size, (k + 1) * size)
        if k == 0:
            to_sib.wait()
            qt[...] = dc[0] * dc[1]
            for d in range(1, chips):
                each = copy(qt, rt.at[d - 1], t_send.at[d - 1], t_recv.at[d - 1], chip_peer(d))
                each.start()
                to_chips[d] = each
        sib_copies[k].wait()
        qb[k, 0] = (dc[1, :, here] * pc[0, k, 0] + pc[1, k, 0]).astype(BF16)
        qb[k, 1] = (pc[0, k, 1] + dc[0, :, here] * pc[1, k, 1]).astype(BF16)
        for d in range(1, chips):
            each = copy(
                qb.at[k, (chip + d) // chips], rq.at[k, d - 1],
                q_send.at[k, d - 1], q_recv.at[k, d - 1], chip_peer(d),
            )
            each.start()
            to_chips[k, d] = each

    summarize(0)
    for k in range(1, parts):
        if k >= early:
            factors(k)
        summarize(k)
        combine(k - 1)
    combine(parts - 1)

    at_r = lax.broadcasted_iota(jnp.int32, (SUB, SUB), 0)
    at_c = lax.broadcasted_iota(jnp.int32, (SUB, SUB), 1)
    b_sums, c_sums = [], []
    for a in range(subs):
        b_a, c_a = b_all[block(a)], c_all[block(a)]
        scores = jnp.where(at_r >= at_c, dot(c_a, b_a, ((1,), (1,))), 0.0).astype(BF16)
        flipped = jnp.where(at_r <= at_c, dot(b_a, c_a, ((1,), (1,))), 0.0).astype(BF16)
        od_s[block(a)] = dot(scores, vx_s[block(a)])
        gd_s[block(a)] = dot(flipped, ug_s[block(a)])
        paired = dot(ug_s[block(a)], vx_s[block(a)], ((1,), (1,)))
        paired = jnp.where(at_r >= at_c, paired, 0.0)
        b_sums.append(split_dot(paired.T, c_a))
        c_sums.append(split_dot(paired, b_a))

    back = [
        copy(tmp.at[other, k], ef.at[core, k], e_send.at[k], e_recv.at[k], sib)
        for k in range(parts)
    ]

    def enter(k):
        here = slice(k * size, (k + 1) * size)
        for d in range(1, chips):
            if k == 0:
                to_chips[d].wait()
            to_chips[k, d].wait()
        e_in = jnp.zeros((state, size), F32)
        f_in = jnp.zeros((state, size), F32)
        reach = jnp.ones((1, size), F32)
        for d in range(1, chips):
            e_in = e_in + jnp.where(chip >= d, reach, 0.0) * rq[k, d - 1].astype(F32)
            reach = reach * rt[d - 1, :, here]
        reach = jnp.ones((1, size), F32)
        for d in range(chips - 1, 0, -1):
            f_in = f_in + jnp.where(chip < d, reach, 0.0) * rq[k, d - 1].astype(F32)
            reach = reach * rt[d - 1, :, here]
        tmp[0, k, 0] = e_in
        tmp[1, k, 0] = dc[0, :, here] * e_in + pc[0, k, 0]
        tmp[1, k, 1] = f_in
        tmp[0, k, 1] = dc[1, :, here] * f_in + pc[1, k, 1]
        back[k].start()
        ef[core, k] = tmp[core, k]

    def states(k):
        back[k].wait()
        es = {}
        for h in range(2):
            lanes = chunk(h, k)
            e, f = ef[h, k, 0], ef[h, k, 1]
            for a in range(subs):
                r = root(a, lanes)
                es[h, a, 0] = (r * e).astype(BF16)
                if a < subs - 1:
                    e = (r * r) * e + ps_s[a, :, lanes]
            for a in range(subs - 1, -1, -1):
                r = root(a, lanes)
                es[h, a, 1] = (r * f).astype(BF16)
                if a > 0:
                    f = (r * r) * f + as_s[a, :, lanes]
            for a in range(subs):
                b_sums[a] += dot(vx_s[block(a), lanes], es[h, a, 1], ((1,), (1,)))
                c_sums[a] += dot(ug_s[block(a), lanes], es[h, a, 0], ((1,), (1,)))
        return es

    stores = []

    def outputs(k, es):
        for h in range(2):
            lanes = chunk(h, k)
            for a in range(subs):
                out = od_s[block(a), lanes] + dot(c_all[block(a)], es[h, a, 0])
                out = u_s[block(a), lanes] * out
                out = out + gain_s[:, lanes] * x_ref[block(a), lanes].astype(F32)
                out_ref[block(a), lanes] = out.astype(BF16)
                grad = gd_s[block(a), lanes] + dot(b_all[block(a)], es[h, a, 1])
                grad = vs_s[block(a), lanes] * grad
                grad = grad + gain_s[:, lanes] * g_ref[block(a), lanes].astype(F32)
                ig_ref[block(a), lanes] = grad.astype(BF16)
            for i, (src, dst) in enumerate([(out_ref, out_hbm), (ig_ref, ig_hbm)]):
                each = pltpu.make_async_copy(src.at[:, lanes], dst.at[:, lanes], o_sem.at[k, h, i])
                each.start()
                stores.append(each)

    enter(0)
    for k in range(1, parts):
        enter(k)
        outputs(k - 1, states(k - 1))
    last = states(parts - 1)
    part[:, 0] = jnp.concatenate(b_sums, axis=0).reshape(zs, rows, state)
    part[:, 1] = jnp.concatenate(c_sums, axis=0).reshape(zs, rows, state)
    scatters = [
        copy(part.at[(z + d) % zs], rpart.at[d - 1], r_send.at[d - 1], r_recv.at[d - 1], z_peer(d))
        for d in range(1, zs)
    ]
    for each in scatters:
        each.start()
    outputs(parts - 1, last)
    gb, gc = part[z, 0], part[z, 1]
    for d, each in enumerate(scatters):
        each.wait()
        gb = gb + rpart[d, 0]
        gc = gc + rpart[d, 1]
    gb_ref[...] = gb
    gc_ref[...] = gc
    for each in stores:
        each.wait()


def local(x_in, b_in, c_in, decay_codes, decay_rate, skip_gain, out_grad):
    tokens, width = x_in.shape
    rows, state = b_in.shape
    heads = decay_codes.shape[0]
    subs = tokens // SUB
    half = width // 2
    parts = max(1, min(4, half // 128))
    size = half // parts
    chips = lax.axis_size("seq") // 2
    zs = lax.axis_size("head")
    vmem = pl.BlockSpec(memory_space=pltpu.VMEM)
    hbm = pl.BlockSpec(memory_space=pltpu.MemorySpace.HBM)
    dma = pltpu.SemaphoreType.DMA
    return pl.pallas_call(
        functools.partial(kernel, chips, zs, parts),
        out_shape=(
            jax.ShapeDtypeStruct((tokens, width), BF16),
            jax.ShapeDtypeStruct((tokens, width), BF16),
            jax.ShapeDtypeStruct((rows, state), F32),
            jax.ShapeDtypeStruct((rows, state), F32),
        ),
        in_specs=[hbm] * 7,
        out_specs=(hbm, hbm, vmem, vmem),
        scratch_shapes=[
            pltpu.VMEM((tokens, width), BF16),
            pltpu.VMEM((tokens, width), BF16),
            pltpu.VMEM((tokens, width), BF16),
            pltpu.VMEM((tokens, width), BF16),
            pltpu.VMEM(decay_codes.shape, jnp.int32),
            pltpu.VMEM((1, heads), F32),
            pltpu.VMEM((1, heads), F32),
            pltpu.VMEM((tokens, width), F32),
            pltpu.VMEM((tokens, width), F32),
            pltpu.VMEM((tokens, width), BF16),
            pltpu.VMEM((tokens, width), BF16),
            pltpu.VMEM((tokens, width), F32),
            pltpu.VMEM((tokens, width), F32),
            pltpu.VMEM((subs, state, width), F32),
            pltpu.VMEM((subs, state, width), F32),
            pltpu.VMEM((1, width), F32),
            pltpu.VMEM((3 * heads, width), BF16),
            pltpu.VMEM((zs, 2, rows, state), BF16),
            pltpu.VMEM((2, parts, 2, state, size), F32),
            pltpu.VMEM((2, 1, half), F32),
            pltpu.VMEM((2, parts, 2, state, size), F32),
            pltpu.VMEM((2, 1, half), F32),
            pltpu.VMEM((parts, 2, state, size), BF16),
            pltpu.VMEM((1, half), F32),
            pltpu.VMEM((parts, chips - 1, state, size), BF16),
            pltpu.VMEM((chips - 1, 1, half), F32),
            pltpu.VMEM((2, parts, 2, state, size), F32),
            pltpu.VMEM((2, parts, 2, state, size), F32),
            pltpu.VMEM((zs, 2, rows, state), F32),
            pltpu.VMEM((zs - 1, 2, rows, state), F32),
            dma((7,)),
            dma((zs - 1,)), dma((zs - 1,)),
            dma((1,)), dma((1,)),
            dma((parts,)), dma((parts,)),
            dma((parts,)), dma((parts,)),
            dma((parts, chips - 1)), dma((parts, chips - 1)),
            dma((chips - 1,)), dma((chips - 1,)),
            dma((zs - 1,)), dma((zs - 1,)),
            dma((parts, 2, 2)),
        ],
        compiler_params=pltpu.CompilerParams(
            collective_id=0, has_side_effects=True, vmem_limit_bytes=61 * 1024 * 1024
        ),
    )(
        x_in, b_in, c_in, decay_codes,
        decay_rate.reshape(1, heads), skip_gain.reshape(1, heads), out_grad,
    )


def solution(mesh):
    placed = (
        P("seq", "head"),
        P(("seq", "head"), None),
        P(("seq", "head"), None),
        P("head", "seq"),
        P("head"),
        P("head"),
        P("seq", "head"),
    )
    return jax.shard_map(
        local,
        mesh=mesh,
        in_specs=placed,
        out_specs=(
            P("seq", "head"),
            P("seq", "head"),
            P(("seq", "head"), None),
            P(("seq", "head"), None),
        ),
        check_vma=False,
    )
```

```python
import functools

import jax
import jax.numpy as jnp
from jax import lax
from jax.experimental import pallas as pl
from jax.experimental.pallas import tpu as pltpu
from jax.sharding import PartitionSpec as P

SUB = 128
MESH = pl.DeviceIdType.MESH
F32 = jnp.float32
BF16 = jnp.bfloat16


def dot(a, b, dims=((1,), (0,))):
    return lax.dot_general(a, b, (dims, ((), ())), preferred_element_type=F32)


def split3(a):
    hi = a.astype(BF16).astype(F32)
    mid = (a - hi).astype(BF16).astype(F32)
    low = a - hi - mid
    return jnp.concatenate([hi, mid, low], axis=0)


def split_dot(a, b, dims=((1,), (0,))):
    hi = a.astype(BF16)
    low = (a - hi.astype(F32)).astype(BF16)
    return dot(hi, b, dims) + dot(low, b, dims)


def kernel(
    chips, zs, parts,
    x_hbm, b_hbm, c_hbm, codes_hbm, rate_hbm, gain_hbm, g_hbm,
    out_hbm, ig_hbm, gb_ref, gc_ref,
    out_ref, ig_ref, x_ref, g_ref, codes_ref, rate_ref, gain_ref,
    u_s, vs_s, ug_s, vx_s, od_s, gd_s, ps_s, as_s, gain_s, spread_s,
    bc, pa, dd, pc, dc, qb, qt, rq, rt, tmp, ef, part, rpart, late, lpart, rlate,
    l_sem, g_send, g_recv, d_send, d_recv, s_send, s_recv, e_send, e_recv,
    q_send, q_recv, t_send, t_recv, r_send, r_recv, w_send, w_recv, o_sem,
):
    tokens, width = x_ref.shape
    heads = codes_ref.shape[0]
    dim = width // heads
    rows, state = b_hbm.shape
    subs = tokens // SUB
    half = width // 2
    size = half // parts
    seq = lax.axis_index("seq")
    z = lax.axis_index("head")
    chip = seq // 2
    core = seq % 2
    other = 1 - core
    sib = {"seq": chip * 2 + other, "head": z}

    def z_peer(d):
        return {"seq": seq, "head": (z + d) % zs}

    def chip_peer(d):
        return {"seq": ((chip + d) % chips) * 2 + core, "head": z}

    def copy(src, dst, send, recv, to):
        return pltpu.make_async_remote_copy(
            src_ref=src, dst_ref=dst, send_sem=send, recv_sem=recv,
            device_id=to, device_id_type=MESH,
        )

    loads = [
        pltpu.make_async_copy(src, dst, l_sem.at[i])
        for i, (src, dst) in enumerate([
            (codes_hbm, codes_ref), (rate_hbm, rate_ref), (gain_hbm, gain_ref),
            (b_hbm, bc.at[z, 0]), (c_hbm, bc.at[z, 1]), (g_hbm, g_ref), (x_hbm, x_ref),
        ])
    ]
    for each in loads:
        each.start()
    barrier = pltpu.get_barrier_semaphore()
    for d in range(1, zs):
        pl.semaphore_signal(barrier, inc=1, device_id=z_peer(d), device_id_type=MESH)
    for d in range(1, chips):
        pl.semaphore_signal(barrier, inc=1, device_id=chip_peer(d), device_id_type=MESH)
    pl.semaphore_signal(barrier, inc=1, device_id=sib, device_id_type=MESH)
    for each in loads[:5]:
        each.wait()
    pl.semaphore_wait(barrier, zs + chips - 1)
    gathers = [
        copy(bc.at[z], bc.at[z], g_send.at[d - 1], g_recv.at[d - 1], z_peer(d))
        for d in range(1, zs)
    ]
    for each in gathers:
        each.start()

    eye = lax.broadcasted_iota(jnp.int32, (heads, heads), 0) == lax.broadcasted_iota(
        jnp.int32, (heads, heads), 1
    )
    rate = jnp.sum(jnp.where(eye, rate_ref[...], 0.0), axis=1, keepdims=True)
    gain = jnp.sum(jnp.where(eye, gain_ref[...], 0.0), axis=1, keepdims=True)
    codes = codes_ref[...]
    step = 0.5 + (codes & 1023).astype(F32) * (1.0 / 1024.0)
    log_decay = -rate * step - 0.1 * (codes >> 10).astype(F32)
    at_u = lax.broadcasted_iota(jnp.int32, (tokens, tokens), 0)
    at_t = lax.broadcasted_iota(jnp.int32, (tokens, tokens), 1)
    centred = jnp.where(
        at_u // SUB == at_t // SUB, jnp.where(at_u <= at_t, 0.5, -0.5), 0.0
    ).astype(BF16)
    logs = dot(split3(log_decay).astype(BF16), centred)
    logs = logs[:heads] + logs[heads : 2 * heads] + logs[2 * heads :]
    u3 = split3(jnp.exp(logs)).T.astype(BF16)
    v3 = split3(jnp.exp(-logs) * step).T.astype(BF16)
    lane = lax.broadcasted_iota(jnp.int32, (heads, width), 1)
    first = lax.broadcasted_iota(jnp.int32, (heads, width), 0) * dim
    own = (lane >= first) & (lane < first + dim)
    gain_s[...] = jnp.sum(jnp.where(own, gain, 0.0), axis=0, keepdims=True)
    ends = [
        jnp.exp(jnp.sum(log_decay, axis=1, keepdims=True)),
        jnp.exp(logs[:, SUB - 1 : SUB]),
        jnp.exp(logs[:, tokens - 1 :]),
    ]
    for i, end in enumerate(ends):
        end = jnp.sum(jnp.where(own, end, 0.0), axis=0, keepdims=True)
        dd[0, i] = end[:, :half]
        dd[1, i] = end[:, half:]
    spread_s[...] = jnp.concatenate([own.astype(F32)] * 3, axis=0).astype(BF16)
    to_sib = copy(dd.at[other], dc.at[core], d_send.at[0], d_recv.at[0], sib)
    to_sib.start()
    dc[core] = dd[core]
    for each in loads[5:]:
        each.wait()

    def block(a):
        return slice(a * SUB, (a + 1) * SUB)

    def chunk(h, k):
        return slice(h * half + k * size, h * half + (k + 1) * size)

    def root(a, lanes):
        return u_s[(a + 1) * SUB - 1 : (a + 1) * SUB, lanes]

    def factors(k):
        for h in range(2):
            lanes = chunk(h, k)
            u = dot(u3, spread_s[:, lanes])
            vs = dot(v3, spread_s[:, lanes])
            u_s[:, lanes] = u
            vs_s[:, lanes] = vs
            ug_s[:, lanes] = (u * g_ref[:, lanes].astype(F32)).astype(BF16)
            vx_s[:, lanes] = (vs * x_ref[:, lanes].astype(F32)).astype(BF16)

    early = parts
    for k in range(early):
        factors(k)
    for each in gathers:
        each.wait()
    b_all = bc[:, 0].reshape(tokens, state)
    c_all = bc[:, 1].reshape(tokens, state)
    b_flip = b_all.astype(F32).T.astype(BF16)
    c_flip = c_all.astype(F32).T.astype(BF16)

    sib_copies = [
        copy(pa.at[other, k], pc.at[core, k], s_send.at[k], s_recv.at[k], sib)
        for k in range(parts)
    ]

    def summarize(k):
        for h in range(2):
            lanes = chunk(h, k)
            total = None
            for a in range(subs):
                r = root(a, lanes)
                ps = r * dot(b_flip[:, block(a)], vx_s[block(a), lanes])
                ad = r * dot(c_flip[:, block(a)], ug_s[block(a), lanes])
                ps_s[a, :, lanes] = ps
                as_s[a, :, lanes] = ad
                if a == 0:
                    p_dev, a_dev, total = ps, ad, r * r
                else:
                    p_dev = (r * r) * p_dev + ps
                    a_dev = a_dev + total * ad
                    total = total * (r * r)
            pa[h, k, 0] = p_dev
            pa[h, k, 1] = a_dev
        sib_copies[k].start()
        pc[core, k] = pa[core, k]

    to_chips = {}

    def combine(k):
        here = slice(k * size, (k + 1) * size)
        if k == 0:
            to_sib.wait()
            qt[...] = dc[0, 0] * dc[1, 0]
            for d in range(1, chips):
                each = copy(qt, rt.at[d - 1], t_send.at[d - 1], t_recv.at[d - 1], chip_peer(d))
                each.start()
                to_chips[d] = each
        sib_copies[k].wait()
        qb[k, 0] = (dc[1, 0, :, here] * pc[0, k, 0] + pc[1, k, 0]).astype(BF16)
        qb[k, 1] = (pc[0, k, 1] + dc[0, 0, :, here] * pc[1, k, 1]).astype(BF16)
        for d in range(1, chips):
            each = copy(
                qb.at[k, (chip + d) // chips], rq.at[k, d - 1],
                q_send.at[k, d - 1], q_recv.at[k, d - 1], chip_peer(d),
            )
            each.start()
            to_chips[k, d] = each

    summarize(0)
    for k in range(1, parts):
        if k >= early:
            factors(k)
        summarize(k)
        combine(k - 1)
    combine(parts - 1)

    at_r = lax.broadcasted_iota(jnp.int32, (SUB, SUB), 0)
    at_c = lax.broadcasted_iota(jnp.int32, (SUB, SUB), 1)
    b_sums, c_sums = [], []
    for a in range(subs):
        b_a, c_a = b_all[block(a)], c_all[block(a)]
        scores = jnp.where(at_r >= at_c, dot(c_a, b_a, ((1,), (1,))), 0.0).astype(BF16)
        flipped = jnp.where(at_r <= at_c, dot(b_a, c_a, ((1,), (1,))), 0.0).astype(BF16)
        od_s[block(a)] = dot(scores, vx_s[block(a)])
        gd_s[block(a)] = dot(flipped, ug_s[block(a)])
        paired = dot(ug_s[block(a)], vx_s[block(a)], ((1,), (1,)))
        paired = jnp.where(at_r >= at_c, paired, 0.0)
        b_sums.append(split_dot(paired.T, c_a))
        c_sums.append(split_dot(paired, b_a))

    back = [
        copy(tmp.at[other, k], ef.at[core, k], e_send.at[k], e_recv.at[k], sib)
        for k in range(parts)
    ]

    def enter(k):
        here = slice(k * size, (k + 1) * size)
        for d in range(1, chips):
            if k == 0:
                to_chips[d].wait()
            to_chips[k, d].wait()
        e_in = jnp.zeros((state, size), F32)
        f_in = jnp.zeros((state, size), F32)
        reach = jnp.ones((1, size), F32)
        for d in range(1, chips):
            e_in = e_in + jnp.where(chip >= d, reach, 0.0) * rq[k, d - 1].astype(F32)
            reach = reach * rt[d - 1, :, here]
        reach = jnp.ones((1, size), F32)
        for d in range(chips - 1, 0, -1):
            f_in = f_in + jnp.where(chip < d, reach, 0.0) * rq[k, d - 1].astype(F32)
            reach = reach * rt[d - 1, :, here]
        e_out = dc[0, 0, :, here] * e_in + pc[0, k, 0]
        f_out = dc[1, 0, :, here] * f_in + pc[1, k, 1]
        tmp[0, k, 0] = (dc[0, 1, :, here] * e_in).astype(BF16)
        tmp[1, k, 0] = (dc[1, 1, :, here] * e_out).astype(BF16)
        tmp[1, k, 1] = (dc[1, 2, :, here] * f_in).astype(BF16)
        tmp[0, k, 1] = (dc[0, 2, :, here] * f_out).astype(BF16)
        back[k].start()
        ef[core, k] = tmp[core, k]

    def states(k):
        back[k].wait()
        es = {}
        for h in range(2):
            lanes = chunk(h, k)
            es[h, 0, 0] = ef[h, k, 0]
            es[h, subs - 1, 1] = ef[h, k, 1]
            e = ef[h, k, 0].astype(F32)
            for a in range(1, subs):
                r = root(a, lanes)
                e = r * (root(a - 1, lanes) * e + ps_s[a - 1, :, lanes])
                es[h, a, 0] = e.astype(BF16)
            f = ef[h, k, 1].astype(F32)
            for a in range(subs - 2, -1, -1):
                r = root(a, lanes)
                f = r * (root(a + 1, lanes) * f + as_s[a + 1, :, lanes])
                es[h, a, 1] = f.astype(BF16)
            for a in range(subs):
                b_sums[a] += dot(vx_s[block(a), lanes], es[h, a, 1], ((1,), (1,)))
                c_sums[a] += dot(ug_s[block(a), lanes], es[h, a, 0], ((1,), (1,)))
        return es

    stores = []

    def outputs(k, es):
        for h in range(2):
            lanes = chunk(h, k)
            for a in range(subs):
                out = od_s[block(a), lanes] + dot(c_all[block(a)], es[h, a, 0])
                out = u_s[block(a), lanes] * out
                out = out + gain_s[:, lanes] * x_ref[block(a), lanes].astype(F32)
                out_ref[block(a), lanes] = out.astype(BF16)
                grad = gd_s[block(a), lanes] + dot(b_all[block(a)], es[h, a, 1])
                grad = vs_s[block(a), lanes] * grad
                grad = grad + gain_s[:, lanes] * g_ref[block(a), lanes].astype(F32)
                ig_ref[block(a), lanes] = grad.astype(BF16)
            for i, (src, dst) in enumerate([(out_ref, out_hbm), (ig_ref, ig_hbm)]):
                each = pltpu.make_async_copy(src.at[:, lanes], dst.at[:, lanes], o_sem.at[k, h, i])
                each.start()
                stores.append(each)

    def scatter(src, dst, send, recv):
        copies = [
            copy(src.at[(z + d) % zs], dst.at[d - 1], send.at[d - 1], recv.at[d - 1], z_peer(d))
            for d in range(1, zs)
        ]
        for each in copies:
            each.start()
        return copies

    def scatter_early():
        part[:, 0] = jnp.concatenate(b_sums, axis=0).reshape(zs, rows, state)
        part[:, 1] = jnp.concatenate(c_sums, axis=0).reshape(zs, rows, state)
        for a in range(subs):
            b_sums[a] = jnp.zeros((SUB, state), F32)
            c_sums[a] = jnp.zeros((SUB, state), F32)
        return scatter(part, rpart, r_send, r_recv)

    if parts < 3:
        sent = scatter_early()
    enter(0)
    for k in range(1, parts):
        enter(k)
        es = states(k - 1)
        if k == parts - 2:
            sent = scatter_early()
        outputs(k - 1, es)
    es = states(parts - 1)
    late[:, 0] = jnp.concatenate(b_sums, axis=0).reshape(zs, rows, state)
    late[:, 1] = jnp.concatenate(c_sums, axis=0).reshape(zs, rows, state)
    lpart[...] = late[...].astype(BF16)
    sent_late = scatter(lpart, rlate, w_send, w_recv)
    outputs(parts - 1, es)
    gb = part[z, 0] + late[z, 0]
    gc = part[z, 1] + late[z, 1]
    for d in range(zs - 1):
        sent[d].wait()
        gb = gb + rpart[d, 0]
        gc = gc + rpart[d, 1]
    for d in range(zs - 1):
        sent_late[d].wait()
        gb = gb + rlate[d, 0].astype(F32)
        gc = gc + rlate[d, 1].astype(F32)
    gb_ref[...] = gb
    gc_ref[...] = gc
    for each in stores:
        each.wait()


def hand_over(*refs):
    count = (len(refs) - 1) // 2
    sems = refs[-1]
    copies = []
    for i in range(count):
        src, dst = refs[i], refs[count + i]
        rows = src.shape[0] // 4
        for j in range(4):
            here = pl.ds(j * rows, rows)
            copies.append(pltpu.make_async_copy(src.at[here], dst.at[here], sems.at[i, j]))
    for each in copies:
        each.start()
    for each in copies:
        each.wait()


def local(x_in, b_in, c_in, decay_codes, decay_rate, skip_gain, out_grad):
    tokens, width = x_in.shape
    rows, state = b_in.shape
    heads = decay_codes.shape[0]
    subs = tokens // SUB
    half = width // 2
    parts = max(1, min(4, half // 128))
    size = half // parts
    chips = lax.axis_size("seq") // 2
    zs = lax.axis_size("head")
    vmem = pl.BlockSpec(memory_space=pltpu.VMEM)
    hbm = pl.BlockSpec(memory_space=pltpu.MemorySpace.HBM)
    dma = pltpu.SemaphoreType.DMA
    results = pl.pallas_call(
        functools.partial(kernel, chips, zs, parts),
        out_shape=(
            jax.ShapeDtypeStruct((tokens, width), BF16),
            jax.ShapeDtypeStruct((tokens, width), BF16),
            jax.ShapeDtypeStruct((rows, state), F32),
            jax.ShapeDtypeStruct((rows, state), F32),
        ),
        in_specs=[hbm] * 7,
        out_specs=(hbm, hbm, vmem, vmem),
        scratch_shapes=[
            pltpu.VMEM((tokens, width), BF16),
            pltpu.VMEM((tokens, width), BF16),
            pltpu.VMEM((tokens, width), BF16),
            pltpu.VMEM((tokens, width), BF16),
            pltpu.VMEM(decay_codes.shape, jnp.int32),
            pltpu.VMEM((1, heads), F32),
            pltpu.VMEM((1, heads), F32),
            pltpu.VMEM((tokens, width), F32),
            pltpu.VMEM((tokens, width), F32),
            pltpu.VMEM((tokens, width), BF16),
            pltpu.VMEM((tokens, width), BF16),
            pltpu.VMEM((tokens, width), F32),
            pltpu.VMEM((tokens, width), F32),
            pltpu.VMEM((subs, state, width), F32),
            pltpu.VMEM((subs, state, width), F32),
            pltpu.VMEM((1, width), F32),
            pltpu.VMEM((3 * heads, width), BF16),
            pltpu.VMEM((zs, 2, rows, state), BF16),
            pltpu.VMEM((2, parts, 2, state, size), F32),
            pltpu.VMEM((2, 3, 1, half), F32),
            pltpu.VMEM((2, parts, 2, state, size), F32),
            pltpu.VMEM((2, 3, 1, half), F32),
            pltpu.VMEM((parts, 2, state, size), BF16),
            pltpu.VMEM((1, half), F32),
            pltpu.VMEM((parts, chips - 1, state, size), BF16),
            pltpu.VMEM((chips - 1, 1, half), F32),
            pltpu.VMEM((2, parts, 2, state, size), BF16),
            pltpu.VMEM((2, parts, 2, state, size), BF16),
            pltpu.VMEM((zs, 2, rows, state), F32),
            pltpu.VMEM((zs - 1, 2, rows, state), F32),
            pltpu.VMEM((zs, 2, rows, state), F32),
            pltpu.VMEM((zs, 2, rows, state), BF16),
            pltpu.VMEM((zs - 1, 2, rows, state), BF16),
            dma((7,)),
            dma((zs - 1,)), dma((zs - 1,)),
            dma((1,)), dma((1,)),
            dma((parts,)), dma((parts,)),
            dma((parts,)), dma((parts,)),
            dma((parts, chips - 1)), dma((parts, chips - 1)),
            dma((chips - 1,)), dma((chips - 1,)),
            dma((zs - 1,)), dma((zs - 1,)),
            dma((zs - 1,)), dma((zs - 1,)),
            dma((parts, 2, 2)),
        ],
        compiler_params=pltpu.CompilerParams(
            collective_id=0, has_side_effects=True, vmem_limit_bytes=61 * 1024 * 1024
        ),
    )(
        x_in, b_in, c_in, decay_codes,
        decay_rate.reshape(1, heads), skip_gain.reshape(1, heads), out_grad,
    )
    return pl.pallas_call(
        hand_over,
        out_shape=tuple(jax.ShapeDtypeStruct(r.shape, r.dtype) for r in results),
        in_specs=[hbm] * 4,
        out_specs=(hbm,) * 4,
        scratch_shapes=[dma((4, 4))],
        compiler_params=pltpu.CompilerParams(vmem_limit_bytes=61 * 1024 * 1024),
    )(*results)


def solution(mesh):
    placed = (
        P("seq", "head"),
        P(("seq", "head"), None),
        P(("seq", "head"), None),
        P("head", "seq"),
        P("head"),
        P("head"),
        P("seq", "head"),
    )
    return jax.shard_map(
        local,
        mesh=mesh,
        in_specs=placed,
        out_specs=(
            P("seq", "head"),
            P("seq", "head"),
            P(("seq", "head"), None),
            P(("seq", "head"), None),
        ),
        check_vma=False,
    )
```

```python
import functools

import jax
import jax.numpy as jnp
from jax import lax
from jax.experimental import pallas as pl
from jax.experimental.pallas import tpu as pltpu
from jax.sharding import PartitionSpec as P

SUB = 128
MESH = pl.DeviceIdType.MESH
F32 = jnp.float32
BF16 = jnp.bfloat16


def dot(a, b, dims=((1,), (0,))):
    return lax.dot_general(a, b, (dims, ((), ())), preferred_element_type=F32)


def split3(a):
    hi = a.astype(BF16).astype(F32)
    mid = (a - hi).astype(BF16).astype(F32)
    low = a - hi - mid
    return jnp.concatenate([hi, mid, low], axis=0)


def split_dot(a, b, dims=((1,), (0,))):
    hi = a.astype(BF16)
    low = (a - hi.astype(F32)).astype(BF16)
    return dot(hi, b, dims) + dot(low, b, dims)


def kernel(
    chips, zs, cuts,
    x_hbm, b_hbm, c_hbm, codes_hbm, rate_hbm, gain_hbm, g_hbm,
    out_hbm, ig_hbm, gb_ref, gc_ref,
    out_ref, ig_ref, x_ref, g_ref, codes_ref, rate_ref, gain_ref,
    u_s, vs_s, ug_s, vx_s, od_s, gd_s, ps_s, as_s, gain_s, spread_s,
    bc, pa, dd, pc, dc, qb, qt, rq, rt, tmp, ef, part, rpart, late, lpart, rlate,
    l_sem, g_send, g_recv, d_send, d_recv, s_send, s_recv, e_send, e_recv,
    q_send, q_recv, t_send, t_recv, r_send, r_recv, w_send, w_recv, o_sem,
):
    tokens, width = x_ref.shape
    heads = codes_ref.shape[0]
    dim = width // heads
    rows, state = b_hbm.shape
    subs = tokens // SUB
    half = width // 2
    parts = len(cuts)
    seq = lax.axis_index("seq")
    z = lax.axis_index("head")
    chip = seq // 2
    core = seq % 2
    other = 1 - core
    sib = {"seq": chip * 2 + other, "head": z}

    def z_peer(d):
        return {"seq": seq, "head": (z + d) % zs}

    def chip_peer(d):
        return {"seq": ((chip + d) % chips) * 2 + core, "head": z}

    def copy(src, dst, send, recv, to):
        return pltpu.make_async_remote_copy(
            src_ref=src, dst_ref=dst, send_sem=send, recv_sem=recv,
            device_id=to, device_id_type=MESH,
        )

    loads = [
        pltpu.make_async_copy(src, dst, l_sem.at[i])
        for i, (src, dst) in enumerate([
            (codes_hbm, codes_ref), (rate_hbm, rate_ref), (gain_hbm, gain_ref),
            (b_hbm, bc.at[z, 0]), (c_hbm, bc.at[z, 1]), (g_hbm, g_ref), (x_hbm, x_ref),
        ])
    ]
    for each in loads:
        each.start()
    barrier = pltpu.get_barrier_semaphore()
    for d in range(1, zs):
        pl.semaphore_signal(barrier, inc=1, device_id=z_peer(d), device_id_type=MESH)
    for d in range(1, chips):
        pl.semaphore_signal(barrier, inc=1, device_id=chip_peer(d), device_id_type=MESH)
    pl.semaphore_signal(barrier, inc=1, device_id=sib, device_id_type=MESH)
    for each in loads[:5]:
        each.wait()
    pl.semaphore_wait(barrier, zs + chips - 1)
    gathers = [
        copy(bc.at[z], bc.at[z], g_send.at[d - 1], g_recv.at[d - 1], z_peer(d))
        for d in range(1, zs)
    ]
    for each in gathers:
        each.start()

    eye = lax.broadcasted_iota(jnp.int32, (heads, heads), 0) == lax.broadcasted_iota(
        jnp.int32, (heads, heads), 1
    )
    rate = jnp.sum(jnp.where(eye, rate_ref[...], 0.0), axis=1, keepdims=True)
    gain = jnp.sum(jnp.where(eye, gain_ref[...], 0.0), axis=1, keepdims=True)
    codes = codes_ref[...]
    step = 0.5 + (codes & 1023).astype(F32) * (1.0 / 1024.0)
    log_decay = -rate * step - 0.1 * (codes >> 10).astype(F32)
    at_u = lax.broadcasted_iota(jnp.int32, (tokens, tokens), 0)
    at_t = lax.broadcasted_iota(jnp.int32, (tokens, tokens), 1)
    centred = jnp.where(
        at_u // SUB == at_t // SUB, jnp.where(at_u <= at_t, 0.5, -0.5), 0.0
    ).astype(BF16)
    logs = dot(split3(log_decay).astype(BF16), centred)
    logs = logs[:heads] + logs[heads : 2 * heads] + logs[2 * heads :]
    u3 = split3(jnp.exp(logs)).T.astype(BF16)
    v3 = split3(jnp.exp(-logs) * step).T.astype(BF16)
    lane = lax.broadcasted_iota(jnp.int32, (heads, width), 1)
    first = lax.broadcasted_iota(jnp.int32, (heads, width), 0) * dim
    own = (lane >= first) & (lane < first + dim)
    gain_s[...] = jnp.sum(jnp.where(own, gain, 0.0), axis=0, keepdims=True)
    ends = [
        jnp.exp(jnp.sum(log_decay, axis=1, keepdims=True)),
        jnp.exp(logs[:, SUB - 1 : SUB]),
        jnp.exp(logs[:, tokens - 1 :]),
    ]
    for i, end in enumerate(ends):
        end = jnp.sum(jnp.where(own, end, 0.0), axis=0, keepdims=True)
        dd[0, i] = end[:, :half]
        dd[1, i] = end[:, half:]
    spread_s[...] = jnp.concatenate([own.astype(F32)] * 3, axis=0).astype(BF16)
    to_sib = copy(dd.at[other], dc.at[core], d_send.at[0], d_recv.at[0], sib)
    to_sib.start()
    dc[core] = dd[core]
    for each in loads[5:]:
        each.wait()

    def block(a):
        return slice(a * SUB, (a + 1) * SUB)

    def chunk(h, k):
        return slice(h * half + cuts[k][0], h * half + cuts[k][1])

    def root(a, lanes):
        return u_s[(a + 1) * SUB - 1 : (a + 1) * SUB, lanes]

    def factors(k):
        for h in range(2):
            lanes = chunk(h, k)
            u = dot(u3, spread_s[:, lanes])
            vs = dot(v3, spread_s[:, lanes])
            u_s[:, lanes] = u
            vs_s[:, lanes] = vs
            ug_s[:, lanes] = (u * g_ref[:, lanes].astype(F32)).astype(BF16)
            vx_s[:, lanes] = (vs * x_ref[:, lanes].astype(F32)).astype(BF16)

    for k in range(parts):
        factors(k)
    for each in gathers:
        each.wait()
    b_all = bc[:, 0].reshape(tokens, state)
    c_all = bc[:, 1].reshape(tokens, state)
    b_flip = b_all.astype(F32).T.astype(BF16)
    c_flip = c_all.astype(F32).T.astype(BF16)

    sib_copies = [
        copy(pa.at[other, :, :, chunk(0, k)], pc.at[core, :, :, chunk(0, k)], s_send.at[k], s_recv.at[k], sib)
        for k in range(parts)
    ]

    def summarize(k):
        for h in range(2):
            lanes = chunk(h, k)
            total = None
            for a in range(subs):
                r = root(a, lanes)
                ps = r * dot(b_flip[:, block(a)], vx_s[block(a), lanes])
                ad = r * dot(c_flip[:, block(a)], ug_s[block(a), lanes])
                ps_s[a, :, lanes] = ps
                as_s[a, :, lanes] = ad
                if a == 0:
                    p_dev, a_dev, total = ps, ad, r * r
                else:
                    p_dev = (r * r) * p_dev + ps
                    a_dev = a_dev + total * ad
                    total = total * (r * r)
            pa[h, 0, :, chunk(0, k)] = p_dev
            pa[h, 1, :, chunk(0, k)] = a_dev
        sib_copies[k].start()
        pc[core, :, :, chunk(0, k)] = pa[core, :, :, chunk(0, k)]

    to_chips = {}

    def combine(k):
        here = chunk(0, k)
        if k == 0:
            to_sib.wait()
            qt[...] = dc[0, 0] * dc[1, 0]
            for d in range(1, chips):
                each = copy(qt, rt.at[d - 1], t_send.at[d - 1], t_recv.at[d - 1], chip_peer(d))
                each.start()
                to_chips[d] = each
        sib_copies[k].wait()
        qb[0, :, here] = (dc[1, 0, :, here] * pc[0, 0, :, here] + pc[1, 0, :, here]).astype(BF16)
        qb[1, :, here] = (pc[0, 1, :, here] + dc[0, 0, :, here] * pc[1, 1, :, here]).astype(BF16)
        for d in range(1, chips):
            each = copy(
                qb.at[(chip + d) // chips, :, here], rq.at[d - 1, :, here],
                q_send.at[k, d - 1], q_recv.at[k, d - 1], chip_peer(d),
            )
            each.start()
            to_chips[k, d] = each

    summarize(0)
    for k in range(1, parts):
        summarize(k)
        combine(k - 1)
    combine(parts - 1)

    at_r = lax.broadcasted_iota(jnp.int32, (SUB, SUB), 0)
    at_c = lax.broadcasted_iota(jnp.int32, (SUB, SUB), 1)
    b_sums, c_sums = [], []
    for a in range(subs):
        b_a, c_a = b_all[block(a)], c_all[block(a)]
        scores = jnp.where(at_r >= at_c, dot(c_a, b_a, ((1,), (1,))), 0.0).astype(BF16)
        flipped = jnp.where(at_r <= at_c, dot(b_a, c_a, ((1,), (1,))), 0.0).astype(BF16)
        od_s[block(a)] = dot(scores, vx_s[block(a)])
        gd_s[block(a)] = dot(flipped, ug_s[block(a)])
        paired = dot(ug_s[block(a)], vx_s[block(a)], ((1,), (1,)))
        paired = jnp.where(at_r >= at_c, paired, 0.0)
        b_sums.append(split_dot(paired.T, c_a))
        c_sums.append(split_dot(paired, b_a))

    back = [
        copy(tmp.at[other, :, :, chunk(0, k)], ef.at[core, :, :, chunk(0, k)], e_send.at[k], e_recv.at[k], sib)
        for k in range(parts)
    ]

    def enter(k):
        here = chunk(0, k)
        for d in range(1, chips):
            if k == 0:
                to_chips[d].wait()
            to_chips[k, d].wait()
        size = cuts[k][1] - cuts[k][0]
        e_in = jnp.zeros((state, size), F32)
        f_in = jnp.zeros((state, size), F32)
        reach = jnp.ones((1, size), F32)
        for d in range(1, chips):
            e_in = e_in + jnp.where(chip >= d, reach, 0.0) * rq[d - 1, :, here].astype(F32)
            reach = reach * rt[d - 1, :, here]
        reach = jnp.ones((1, size), F32)
        for d in range(chips - 1, 0, -1):
            f_in = f_in + jnp.where(chip < d, reach, 0.0) * rq[d - 1, :, here].astype(F32)
            reach = reach * rt[d - 1, :, here]
        e_out = dc[0, 0, :, here] * e_in + pc[0, 0, :, here]
        f_out = dc[1, 0, :, here] * f_in + pc[1, 1, :, here]
        tmp[0, 0, :, here] = (dc[0, 1, :, here] * e_in).astype(BF16)
        tmp[1, 0, :, here] = (dc[1, 1, :, here] * e_out).astype(BF16)
        tmp[1, 1, :, here] = (dc[1, 2, :, here] * f_in).astype(BF16)
        tmp[0, 1, :, here] = (dc[0, 2, :, here] * f_out).astype(BF16)
        back[k].start()
        ef[core, :, :, here] = tmp[core, :, :, here]

    def states(k):
        back[k].wait()
        es = {}
        for h in range(2):
            lanes = chunk(h, k)
            es[h, 0, 0] = ef[h, 0, :, chunk(0, k)]
            es[h, subs - 1, 1] = ef[h, 1, :, chunk(0, k)]
            e = ef[h, 0, :, chunk(0, k)].astype(F32)
            for a in range(1, subs):
                r = root(a, lanes)
                e = r * (root(a - 1, lanes) * e + ps_s[a - 1, :, lanes])
                es[h, a, 0] = e.astype(BF16)
            f = ef[h, 1, :, chunk(0, k)].astype(F32)
            for a in range(subs - 2, -1, -1):
                r = root(a, lanes)
                f = r * (root(a + 1, lanes) * f + as_s[a + 1, :, lanes])
                es[h, a, 1] = f.astype(BF16)
            for a in range(subs):
                b_sums[a] += dot(vx_s[block(a), lanes], es[h, a, 1], ((1,), (1,)))
                c_sums[a] += dot(ug_s[block(a), lanes], es[h, a, 0], ((1,), (1,)))
        return es

    stores = []

    def outputs(k, es):
        for h in range(2):
            lanes = chunk(h, k)
            for a in range(subs):
                out = od_s[block(a), lanes] + dot(c_all[block(a)], es[h, a, 0])
                out = u_s[block(a), lanes] * out
                out = out + gain_s[:, lanes] * x_ref[block(a), lanes].astype(F32)
                out_ref[block(a), lanes] = out.astype(BF16)
                grad = gd_s[block(a), lanes] + dot(b_all[block(a)], es[h, a, 1])
                grad = vs_s[block(a), lanes] * grad
                grad = grad + gain_s[:, lanes] * g_ref[block(a), lanes].astype(F32)
                ig_ref[block(a), lanes] = grad.astype(BF16)
            for i, (src, dst) in enumerate([(out_ref, out_hbm), (ig_ref, ig_hbm)]):
                each = pltpu.make_async_copy(src.at[:, lanes], dst.at[:, lanes], o_sem.at[k, h, i])
                each.start()
                stores.append(each)

    def scatter(src, dst, send, recv):
        copies = [
            copy(src.at[(z + d) % zs], dst.at[d - 1], send.at[d - 1], recv.at[d - 1], z_peer(d))
            for d in range(1, zs)
        ]
        for each in copies:
            each.start()
        return copies

    def scatter_early():
        part[:, 0] = jnp.concatenate(b_sums, axis=0).reshape(zs, rows, state)
        part[:, 1] = jnp.concatenate(c_sums, axis=0).reshape(zs, rows, state)
        for a in range(subs):
            b_sums[a] = jnp.zeros((SUB, state), F32)
            c_sums[a] = jnp.zeros((SUB, state), F32)
        return scatter(part, rpart, r_send, r_recv)

    early = parts - 4
    if early < 0:
        sent = scatter_early()
    enter(0)
    for k in range(1, parts):
        enter(k)
        es = states(k - 1)
        if k - 1 == early:
            sent = scatter_early()
        outputs(k - 1, es)
    es = states(parts - 1)
    late[:, 0] = jnp.concatenate(b_sums, axis=0).reshape(zs, rows, state)
    late[:, 1] = jnp.concatenate(c_sums, axis=0).reshape(zs, rows, state)
    lpart[...] = late[...].astype(BF16)
    sent_late = scatter(lpart, rlate, w_send, w_recv)
    outputs(parts - 1, es)
    gb = part[z, 0] + late[z, 0]
    gc = part[z, 1] + late[z, 1]
    for d in range(zs - 1):
        sent[d].wait()
        gb = gb + rpart[d, 0]
        gc = gc + rpart[d, 1]
    for d in range(zs - 1):
        sent_late[d].wait()
        gb = gb + rlate[d, 0].astype(F32)
        gc = gc + rlate[d, 1].astype(F32)
    gb_ref[...] = gb
    gc_ref[...] = gc
    for each in stores:
        each.wait()


def chunks(half):
    units = half // 128
    sizes = [1] * units
    if units >= 4:
        sizes = [1] + [2] * ((units - 2) // 2) + [1] * (1 + units % 2)
    cuts, at = [], 0
    for size in sizes:
        cuts.append((at, at + 128 * size))
        at += 128 * size
    return cuts


def hand_over(*refs):
    count = (len(refs) - 2) // 3
    sems_in, sems_out = refs[-2:]
    loads, stores = [], []
    for i in range(count):
        src, dst, held = refs[i], refs[count + i], refs[2 * count + i]
        rows = src.shape[0] // 4
        for j in range(4):
            here = pl.ds(j * rows, rows)
            loads.append(pltpu.make_async_copy(src.at[here], held.at[here], sems_in.at[i, j]))
            stores.append(pltpu.make_async_copy(held.at[here], dst.at[here], sems_out.at[i, j]))
    for each in loads:
        each.start()
    for load, store in zip(loads, stores):
        load.wait()
        store.start()
    for each in stores:
        each.wait()


def local(x_in, b_in, c_in, decay_codes, decay_rate, skip_gain, out_grad):
    tokens, width = x_in.shape
    rows, state = b_in.shape
    heads = decay_codes.shape[0]
    subs = tokens // SUB
    half = width // 2
    cuts = chunks(half)
    parts = len(cuts)
    chips = lax.axis_size("seq") // 2
    zs = lax.axis_size("head")
    vmem = pl.BlockSpec(memory_space=pltpu.VMEM)
    hbm = pl.BlockSpec(memory_space=pltpu.MemorySpace.HBM)
    dma = pltpu.SemaphoreType.DMA
    results = pl.pallas_call(
        functools.partial(kernel, chips, zs, cuts),
        out_shape=(
            jax.ShapeDtypeStruct((tokens, width), BF16),
            jax.ShapeDtypeStruct((tokens, width), BF16),
            jax.ShapeDtypeStruct((rows, state), F32),
            jax.ShapeDtypeStruct((rows, state), F32),
        ),
        in_specs=[hbm] * 7,
        out_specs=(hbm, hbm, vmem, vmem),
        scratch_shapes=[
            pltpu.VMEM((tokens, width), BF16),
            pltpu.VMEM((tokens, width), BF16),
            pltpu.VMEM((tokens, width), BF16),
            pltpu.VMEM((tokens, width), BF16),
            pltpu.VMEM(decay_codes.shape, jnp.int32),
            pltpu.VMEM((1, heads), F32),
            pltpu.VMEM((1, heads), F32),
            pltpu.VMEM((tokens, width), F32),
            pltpu.VMEM((tokens, width), F32),
            pltpu.VMEM((tokens, width), BF16),
            pltpu.VMEM((tokens, width), BF16),
            pltpu.VMEM((tokens, width), F32),
            pltpu.VMEM((tokens, width), F32),
            pltpu.VMEM((subs, state, width), F32),
            pltpu.VMEM((subs, state, width), F32),
            pltpu.VMEM((1, width), F32),
            pltpu.VMEM((3 * heads, width), BF16),
            pltpu.VMEM((zs, 2, rows, state), BF16),
            pltpu.VMEM((2, 2, state, half), F32),
            pltpu.VMEM((2, 3, 1, half), F32),
            pltpu.VMEM((2, 2, state, half), F32),
            pltpu.VMEM((2, 3, 1, half), F32),
            pltpu.VMEM((2, state, half), BF16),
            pltpu.VMEM((1, half), F32),
            pltpu.VMEM((chips - 1, state, half), BF16),
            pltpu.VMEM((chips - 1, 1, half), F32),
            pltpu.VMEM((2, 2, state, half), BF16),
            pltpu.VMEM((2, 2, state, half), BF16),
            pltpu.VMEM((zs, 2, rows, state), F32),
            pltpu.VMEM((zs - 1, 2, rows, state), F32),
            pltpu.VMEM((zs, 2, rows, state), F32),
            pltpu.VMEM((zs, 2, rows, state), BF16),
            pltpu.VMEM((zs - 1, 2, rows, state), BF16),
            dma((7,)),
            dma((zs - 1,)), dma((zs - 1,)),
            dma((1,)), dma((1,)),
            dma((parts,)), dma((parts,)),
            dma((parts,)), dma((parts,)),
            dma((parts, chips - 1)), dma((parts, chips - 1)),
            dma((chips - 1,)), dma((chips - 1,)),
            dma((zs - 1,)), dma((zs - 1,)),
            dma((zs - 1,)), dma((zs - 1,)),
            dma((parts, 2, 2)),
        ],
        compiler_params=pltpu.CompilerParams(
            collective_id=0, has_side_effects=True, vmem_limit_bytes=61 * 1024 * 1024
        ),
    )(
        x_in, b_in, c_in, decay_codes,
        decay_rate.reshape(1, heads), skip_gain.reshape(1, heads), out_grad,
    )
    return pl.pallas_call(
        hand_over,
        out_shape=tuple(jax.ShapeDtypeStruct(r.shape, r.dtype) for r in results),
        in_specs=[hbm] * 4,
        out_specs=(hbm,) * 4,
        scratch_shapes=[pltpu.VMEM(r.shape, r.dtype) for r in results] + [dma((4, 4)), dma((4, 4))],
        compiler_params=pltpu.CompilerParams(vmem_limit_bytes=61 * 1024 * 1024),
    )(*results)


def solution(mesh):
    placed = (
        P("seq", "head"),
        P(("seq", "head"), None),
        P(("seq", "head"), None),
        P("head", "seq"),
        P("head"),
        P("head"),
        P("seq", "head"),
    )
    return jax.shard_map(
        local,
        mesh=mesh,
        in_specs=placed,
        out_specs=(
            P("seq", "head"),
            P("seq", "head"),
            P(("seq", "head"), None),
            P(("seq", "head"), None),
        ),
        check_vma=False,
    )
```

```python
import functools

import jax
import jax.numpy as jnp
from jax import lax
from jax.experimental import pallas as pl
from jax.experimental.pallas import tpu as pltpu
from jax.sharding import PartitionSpec as P

SUB = 128
MESH = pl.DeviceIdType.MESH
F32 = jnp.float32
BF16 = jnp.bfloat16


def dot(a, b, dims=((1,), (0,))):
    return lax.dot_general(a, b, (dims, ((), ())), preferred_element_type=F32)


def split3(a):
    hi = a.astype(BF16).astype(F32)
    mid = (a - hi).astype(BF16).astype(F32)
    low = a - hi - mid
    return jnp.concatenate([hi, mid, low], axis=0)


def split_dot(a, b, dims=((1,), (0,))):
    hi = a.astype(BF16)
    low = (a - hi.astype(F32)).astype(BF16)
    return dot(hi, b, dims) + dot(low, b, dims)


def kernel(
    chips, zs, cuts,
    x_hbm, b_hbm, c_hbm, codes_hbm, rate_hbm, gain_hbm, g_hbm,
    out_ref, ig_ref, gb_ref, gc_ref,
    x_ref, g_ref, codes_ref, rate_ref, gain_ref,
    u_s, vs_s, ug_s, vx_s, od_s, gd_s, ps_s, as_s, gain_s, spread_s,
    bc, pa, dd, pc, dc, qb, qt, rq, rt, tmp, ef, part, rpart, late, lpart, rlate,
    l_sem, g_send, g_recv, d_send, d_recv, s_send, s_recv, e_send, e_recv,
    q_send, q_recv, t_send, t_recv, r_send, r_recv, w_send, w_recv,
):
    tokens, width = x_ref.shape
    heads = codes_ref.shape[0]
    dim = width // heads
    rows, state = b_hbm.shape
    subs = tokens // SUB
    half = width // 2
    parts = len(cuts)
    seq = lax.axis_index("seq")
    z = lax.axis_index("head")
    chip = seq // 2
    core = seq % 2
    other = 1 - core
    sib = {"seq": chip * 2 + other, "head": z}

    def z_peer(d):
        return {"seq": seq, "head": (z + d) % zs}

    def chip_peer(d):
        return {"seq": ((chip + d) % chips) * 2 + core, "head": z}

    def copy(src, dst, send, recv, to):
        return pltpu.make_async_remote_copy(
            src_ref=src, dst_ref=dst, send_sem=send, recv_sem=recv,
            device_id=to, device_id_type=MESH,
        )

    loads = [
        pltpu.make_async_copy(src, dst, l_sem.at[i])
        for i, (src, dst) in enumerate([
            (codes_hbm, codes_ref), (rate_hbm, rate_ref), (gain_hbm, gain_ref),
            (b_hbm, bc.at[z, 0]), (c_hbm, bc.at[z, 1]), (g_hbm, g_ref), (x_hbm, x_ref),
        ])
    ]
    for each in loads:
        each.start()
    barrier = pltpu.get_barrier_semaphore()
    for d in range(1, zs):
        pl.semaphore_signal(barrier, inc=1, device_id=z_peer(d), device_id_type=MESH)
    for d in range(1, chips):
        pl.semaphore_signal(barrier, inc=1, device_id=chip_peer(d), device_id_type=MESH)
    pl.semaphore_signal(barrier, inc=1, device_id=sib, device_id_type=MESH)
    for each in loads[:3]:
        each.wait()

    eye = lax.broadcasted_iota(jnp.int32, (heads, heads), 0) == lax.broadcasted_iota(
        jnp.int32, (heads, heads), 1
    )
    rate = jnp.sum(jnp.where(eye, rate_ref[...], 0.0), axis=1, keepdims=True)
    gain = jnp.sum(jnp.where(eye, gain_ref[...], 0.0), axis=1, keepdims=True)
    codes = codes_ref[...]
    step = 0.5 + (codes & 1023).astype(F32) * (1.0 / 1024.0)
    log_decay = -rate * step - 0.1 * (codes >> 10).astype(F32)
    at_u = lax.broadcasted_iota(jnp.int32, (tokens, tokens), 0)
    at_t = lax.broadcasted_iota(jnp.int32, (tokens, tokens), 1)
    centred = jnp.where(
        at_u // SUB == at_t // SUB, jnp.where(at_u <= at_t, 0.5, -0.5), 0.0
    ).astype(BF16)
    logs = dot(split3(log_decay).astype(BF16), centred)
    logs = logs[:heads] + logs[heads : 2 * heads] + logs[2 * heads :]
    u3 = split3(jnp.exp(logs)).T.astype(BF16)
    v3 = split3(jnp.exp(-logs) * step).T.astype(BF16)
    lane = lax.broadcasted_iota(jnp.int32, (heads, width), 1)
    first = lax.broadcasted_iota(jnp.int32, (heads, width), 0) * dim
    own = (lane >= first) & (lane < first + dim)
    gain_s[...] = jnp.sum(jnp.where(own, gain, 0.0), axis=0, keepdims=True)
    ends = [
        jnp.exp(jnp.sum(log_decay, axis=1, keepdims=True)),
        jnp.exp(logs[:, SUB - 1 : SUB]),
        jnp.exp(logs[:, tokens - 1 :]),
    ]
    for i, end in enumerate(ends):
        end = jnp.sum(jnp.where(own, end, 0.0), axis=0, keepdims=True)
        dd[0, i] = end[:, :half]
        dd[1, i] = end[:, half:]
    spread_s[...] = jnp.concatenate([own.astype(F32)] * 3, axis=0).astype(BF16)
    for each in loads[3:5]:
        each.wait()
    pl.semaphore_wait(barrier, zs + chips - 1)
    gathers = [
        copy(bc.at[z], bc.at[z], g_send.at[d - 1], g_recv.at[d - 1], z_peer(d))
        for d in range(1, zs)
    ]
    for each in gathers:
        each.start()

    to_sib = copy(dd.at[other], dc.at[core], d_send.at[0], d_recv.at[0], sib)
    to_sib.start()
    dc[core] = dd[core]
    for each in loads[5:]:
        each.wait()

    def block(a):
        return slice(a * SUB, (a + 1) * SUB)

    def chunk(h, k):
        return slice(h * half + cuts[k][0], h * half + cuts[k][1])

    def root(a, lanes):
        return u_s[(a + 1) * SUB - 1 : (a + 1) * SUB, lanes]

    def factors(k):
        for h in range(2):
            lanes = chunk(h, k)
            u = dot(u3, spread_s[:, lanes])
            vs = dot(v3, spread_s[:, lanes])
            u_s[:, lanes] = u
            vs_s[:, lanes] = vs
            ug_s[:, lanes] = (u * g_ref[:, lanes].astype(F32)).astype(BF16)
            vx_s[:, lanes] = (vs * x_ref[:, lanes].astype(F32)).astype(BF16)

    for k in range(parts):
        factors(k)
    for each in gathers:
        each.wait()
    b_all = bc[:, 0].reshape(tokens, state)
    c_all = bc[:, 1].reshape(tokens, state)
    b_flip = b_all.astype(F32).T.astype(BF16)
    c_flip = c_all.astype(F32).T.astype(BF16)

    sib_copies = [
        copy(pa.at[other, :, :, chunk(0, k)], pc.at[core, :, :, chunk(0, k)], s_send.at[k], s_recv.at[k], sib)
        for k in range(parts)
    ]

    def summarize(k):
        for h in range(2):
            lanes = chunk(h, k)
            total = None
            for a in range(subs):
                r = root(a, lanes)
                ps = r * dot(b_flip[:, block(a)], vx_s[block(a), lanes])
                ad = r * dot(c_flip[:, block(a)], ug_s[block(a), lanes])
                ps_s[a, :, lanes] = ps
                as_s[a, :, lanes] = ad
                if a == 0:
                    p_dev, a_dev, total = ps, ad, r * r
                else:
                    p_dev = (r * r) * p_dev + ps
                    a_dev = a_dev + total * ad
                    total = total * (r * r)
            pa[h, 0, :, chunk(0, k)] = p_dev
            pa[h, 1, :, chunk(0, k)] = a_dev
        sib_copies[k].start()
        pc[core, :, :, chunk(0, k)] = pa[core, :, :, chunk(0, k)]

    to_chips = {}

    def combine(k):
        here = chunk(0, k)
        if k == 0:
            to_sib.wait()
            qt[...] = dc[0, 0] * dc[1, 0]
            for d in range(1, chips):
                each = copy(qt, rt.at[d - 1], t_send.at[d - 1], t_recv.at[d - 1], chip_peer(d))
                each.start()
                to_chips[d] = each
        sib_copies[k].wait()
        qb[0, :, here] = (dc[1, 0, :, here] * pc[0, 0, :, here] + pc[1, 0, :, here]).astype(BF16)
        qb[1, :, here] = (pc[0, 1, :, here] + dc[0, 0, :, here] * pc[1, 1, :, here]).astype(BF16)
        for d in range(1, chips):
            each = copy(
                qb.at[(chip + d) // chips, :, here], rq.at[d - 1, :, here],
                q_send.at[k, d - 1], q_recv.at[k, d - 1], chip_peer(d),
            )
            each.start()
            to_chips[k, d] = each

    summarize(0)
    for k in range(1, parts):
        summarize(k)
        combine(k - 1)
    combine(parts - 1)

    at_r = lax.broadcasted_iota(jnp.int32, (SUB, SUB), 0)
    at_c = lax.broadcasted_iota(jnp.int32, (SUB, SUB), 1)
    b_sums, c_sums = [], []
    for a in range(subs):
        b_a, c_a = b_all[block(a)], c_all[block(a)]
        scores = jnp.where(at_r >= at_c, dot(c_a, b_a, ((1,), (1,))), 0.0).astype(BF16)
        flipped = jnp.where(at_r <= at_c, dot(b_a, c_a, ((1,), (1,))), 0.0).astype(BF16)
        od_s[block(a)] = dot(scores, vx_s[block(a)])
        gd_s[block(a)] = dot(flipped, ug_s[block(a)])
        paired = dot(ug_s[block(a)], vx_s[block(a)], ((1,), (1,)))
        paired = jnp.where(at_r >= at_c, paired, 0.0)
        b_sums.append(split_dot(paired.T, c_a))
        c_sums.append(split_dot(paired, b_a))

    back = [
        copy(tmp.at[other, :, :, chunk(0, k)], ef.at[core, :, :, chunk(0, k)], e_send.at[k], e_recv.at[k], sib)
        for k in range(parts)
    ]

    def enter(k):
        here = chunk(0, k)
        for d in range(1, chips):
            if k == 0:
                to_chips[d].wait()
            to_chips[k, d].wait()
        size = cuts[k][1] - cuts[k][0]
        e_in = jnp.zeros((state, size), F32)
        f_in = jnp.zeros((state, size), F32)
        reach = jnp.ones((1, size), F32)
        for d in range(1, chips):
            e_in = e_in + jnp.where(chip >= d, reach, 0.0) * rq[d - 1, :, here].astype(F32)
            reach = reach * rt[d - 1, :, here]
        reach = jnp.ones((1, size), F32)
        for d in range(chips - 1, 0, -1):
            f_in = f_in + jnp.where(chip < d, reach, 0.0) * rq[d - 1, :, here].astype(F32)
            reach = reach * rt[d - 1, :, here]
        e_out = dc[0, 0, :, here] * e_in + pc[0, 0, :, here]
        f_out = dc[1, 0, :, here] * f_in + pc[1, 1, :, here]
        tmp[0, 0, :, here] = (dc[0, 1, :, here] * e_in).astype(BF16)
        tmp[1, 0, :, here] = (dc[1, 1, :, here] * e_out).astype(BF16)
        tmp[1, 1, :, here] = (dc[1, 2, :, here] * f_in).astype(BF16)
        tmp[0, 1, :, here] = (dc[0, 2, :, here] * f_out).astype(BF16)
        back[k].start()
        ef[core, :, :, here] = tmp[core, :, :, here]

    def states(k):
        back[k].wait()
        es = {}
        for h in range(2):
            lanes = chunk(h, k)
            es[h, 0, 0] = ef[h, 0, :, chunk(0, k)]
            es[h, subs - 1, 1] = ef[h, 1, :, chunk(0, k)]
            e = ef[h, 0, :, chunk(0, k)].astype(F32)
            for a in range(1, subs):
                r = root(a, lanes)
                e = r * (root(a - 1, lanes) * e + ps_s[a - 1, :, lanes])
                es[h, a, 0] = e.astype(BF16)
            f = ef[h, 1, :, chunk(0, k)].astype(F32)
            for a in range(subs - 2, -1, -1):
                r = root(a, lanes)
                f = r * (root(a + 1, lanes) * f + as_s[a + 1, :, lanes])
                es[h, a, 1] = f.astype(BF16)
            for a in range(subs):
                b_sums[a] += dot(vx_s[block(a), lanes], es[h, a, 1], ((1,), (1,)))
                c_sums[a] += dot(ug_s[block(a), lanes], es[h, a, 0], ((1,), (1,)))
        return es

    def outputs(k, es):
        for h in range(2):
            lanes = chunk(h, k)
            for a in range(subs):
                out = od_s[block(a), lanes] + dot(c_all[block(a)], es[h, a, 0])
                out = u_s[block(a), lanes] * out
                out = out + gain_s[:, lanes] * x_ref[block(a), lanes].astype(F32)
                out_ref[block(a), lanes] = out.astype(BF16)
                grad = gd_s[block(a), lanes] + dot(b_all[block(a)], es[h, a, 1])
                grad = vs_s[block(a), lanes] * grad
                grad = grad + gain_s[:, lanes] * g_ref[block(a), lanes].astype(F32)
                ig_ref[block(a), lanes] = grad.astype(BF16)

    def scatter(src, dst, send, recv):
        copies = [
            copy(src.at[(z + d) % zs], dst.at[d - 1], send.at[d - 1], recv.at[d - 1], z_peer(d))
            for d in range(1, zs)
        ]
        for each in copies:
            each.start()
        return copies

    def scatter_early():
        part[:, 0] = jnp.concatenate(b_sums, axis=0).reshape(zs, rows, state)
        part[:, 1] = jnp.concatenate(c_sums, axis=0).reshape(zs, rows, state)
        for a in range(subs):
            b_sums[a] = jnp.zeros((SUB, state), F32)
            c_sums[a] = jnp.zeros((SUB, state), F32)
        return scatter(part, rpart, r_send, r_recv)

    early = parts - 4
    if early < 0:
        sent = scatter_early()
    enter(0)
    for k in range(1, parts):
        enter(k)
        es = states(k - 1)
        if k - 1 == early:
            sent = scatter_early()
        outputs(k - 1, es)
    es = states(parts - 1)
    late[:, 0] = jnp.concatenate(b_sums, axis=0).reshape(zs, rows, state)
    late[:, 1] = jnp.concatenate(c_sums, axis=0).reshape(zs, rows, state)
    lpart[...] = late[...].astype(BF16)
    sent_late = scatter(lpart, rlate, w_send, w_recv)
    outputs(parts - 1, es)
    gb = part[z, 0] + late[z, 0]
    gc = part[z, 1] + late[z, 1]
    for d in range(zs - 1):
        sent[d].wait()
        gb = gb + rpart[d, 0]
        gc = gc + rpart[d, 1]
    for d in range(zs - 1):
        sent_late[d].wait()
        gb = gb + rlate[d, 0].astype(F32)
        gc = gc + rlate[d, 1].astype(F32)
    gb_ref[...] = gb
    gc_ref[...] = gc


def chunks(half):
    units = half // 128
    sizes = [1] * units
    if units >= 4:
        sizes = [1] + [2] * ((units - 2) // 2) + [1] * (1 + units % 2)
    cuts, at = [], 0
    for size in sizes:
        cuts.append((at, at + 128 * size))
        at += 128 * size
    return cuts


def hand_over(*refs):
    count = (len(refs) - 1) // 2
    sems = refs[-1]
    copies = []
    for i in range(count):
        src, dst = refs[i], refs[count + i]
        rows = src.shape[0] // 4
        for j in range(4):
            here = pl.ds(j * rows, rows)
            copies.append(pltpu.make_async_copy(src.at[here], dst.at[here], sems.at[i, j]))
    for each in copies:
        each.start()
    for each in copies:
        each.wait()


def local(x_in, b_in, c_in, decay_codes, decay_rate, skip_gain, out_grad):
    tokens, width = x_in.shape
    rows, state = b_in.shape
    heads = decay_codes.shape[0]
    subs = tokens // SUB
    half = width // 2
    cuts = chunks(half)
    parts = len(cuts)
    chips = lax.axis_size("seq") // 2
    zs = lax.axis_size("head")
    vmem = pl.BlockSpec(memory_space=pltpu.VMEM)
    hbm = pl.BlockSpec(memory_space=pltpu.MemorySpace.HBM)
    dma = pltpu.SemaphoreType.DMA
    results = pl.pallas_call(
        functools.partial(kernel, chips, zs, cuts),
        out_shape=(
            pltpu.MemorySpace.VMEM((tokens, width), BF16),
            pltpu.MemorySpace.VMEM((tokens, width), BF16),
            pltpu.MemorySpace.VMEM((rows, state), F32),
            pltpu.MemorySpace.VMEM((rows, state), F32),
        ),
        in_specs=[hbm] * 7,
        out_specs=(vmem,) * 4,
        scratch_shapes=[
            pltpu.VMEM((tokens, width), BF16),
            pltpu.VMEM((tokens, width), BF16),
            pltpu.VMEM(decay_codes.shape, jnp.int32),
            pltpu.VMEM((1, heads), F32),
            pltpu.VMEM((1, heads), F32),
            pltpu.VMEM((tokens, width), F32),
            pltpu.VMEM((tokens, width), F32),
            pltpu.VMEM((tokens, width), BF16),
            pltpu.VMEM((tokens, width), BF16),
            pltpu.VMEM((tokens, width), F32),
            pltpu.VMEM((tokens, width), F32),
            pltpu.VMEM((subs, state, width), F32),
            pltpu.VMEM((subs, state, width), F32),
            pltpu.VMEM((1, width), F32),
            pltpu.VMEM((3 * heads, width), BF16),
            pltpu.VMEM((zs, 2, rows, state), BF16),
            pltpu.VMEM((2, 2, state, half), F32),
            pltpu.VMEM((2, 3, 1, half), F32),
            pltpu.VMEM((2, 2, state, half), F32),
            pltpu.VMEM((2, 3, 1, half), F32),
            pltpu.VMEM((2, state, half), BF16),
            pltpu.VMEM((1, half), F32),
            pltpu.VMEM((chips - 1, state, half), BF16),
            pltpu.VMEM((chips - 1, 1, half), F32),
            pltpu.VMEM((2, 2, state, half), BF16),
            pltpu.VMEM((2, 2, state, half), BF16),
            pltpu.VMEM((zs, 2, rows, state), F32),
            pltpu.VMEM((zs - 1, 2, rows, state), F32),
            pltpu.VMEM((zs, 2, rows, state), F32),
            pltpu.VMEM((zs, 2, rows, state), BF16),
            pltpu.VMEM((zs - 1, 2, rows, state), BF16),
            dma((7,)),
            dma((zs - 1,)), dma((zs - 1,)),
            dma((1,)), dma((1,)),
            dma((parts,)), dma((parts,)),
            dma((parts,)), dma((parts,)),
            dma((parts, chips - 1)), dma((parts, chips - 1)),
            dma((chips - 1,)), dma((chips - 1,)),
            dma((zs - 1,)), dma((zs - 1,)),
            dma((zs - 1,)), dma((zs - 1,)),
        ],
        compiler_params=pltpu.CompilerParams(
            collective_id=0, has_side_effects=True, vmem_limit_bytes=58 * 1024 * 1024
        ),
    )(
        x_in, b_in, c_in, decay_codes,
        decay_rate.reshape(1, heads), skip_gain.reshape(1, heads), out_grad,
    )
    return pl.pallas_call(
        hand_over,
        out_shape=tuple(jax.ShapeDtypeStruct(r.shape, r.dtype) for r in results),
        in_specs=[vmem] * 4,
        out_specs=(hbm,) * 4,
        scratch_shapes=[dma((4, 4))],
        compiler_params=pltpu.CompilerParams(vmem_limit_bytes=4 * 1024 * 1024),
    )(*results)


def solution(mesh):
    placed = (
        P("seq", "head"),
        P(("seq", "head"), None),
        P(("seq", "head"), None),
        P("head", "seq"),
        P("head"),
        P("head"),
        P("seq", "head"),
    )
    return jax.shard_map(
        local,
        mesh=mesh,
        in_specs=placed,
        out_specs=(
            P("seq", "head"),
            P("seq", "head"),
            P(("seq", "head"), None),
            P(("seq", "head"), None),
        ),
        check_vma=False,
    )
```

```python
import functools

import jax
import jax.numpy as jnp
from jax import lax
from jax.experimental import pallas as pl
from jax.experimental.pallas import tpu as pltpu
from jax.sharding import PartitionSpec as P

SUB = 128
MESH = pl.DeviceIdType.MESH
F32 = jnp.float32
BF16 = jnp.bfloat16


def dot(a, b, dims=((1,), (0,))):
    return lax.dot_general(a, b, (dims, ((), ())), preferred_element_type=F32)


def split3(a):
    hi = a.astype(BF16).astype(F32)
    mid = (a - hi).astype(BF16).astype(F32)
    low = a - hi - mid
    return jnp.concatenate([hi, mid, low], axis=0)


def split_dot(a, b, dims=((1,), (0,))):
    hi = a.astype(BF16)
    low = (a - hi.astype(F32)).astype(BF16)
    return dot(hi, b, dims) + dot(low, b, dims)


def kernel(
    chips, zs, cuts,
    x_hbm, b_hbm, c_hbm, codes_hbm, rate_hbm, gain_hbm, g_hbm,
    out_ref, ig_ref, gb_ref, gc_ref,
    x_ref, g_ref, codes_ref, rate_ref, gain_ref,
    u_s, vs_s, ug_s, vx_s, od_s, gd_s, ps_s, as_s, gain_s, spread_s,
    bc, pa, dd, pc, dc, qb, qt, rq, rt, tmp, ef, part, rpart, late, lpart, rlate,
    l_sem, g_send, g_recv, d_send, d_recv, s_send, s_recv, e_send, e_recv,
    q_send, q_recv, t_send, t_recv, r_send, r_recv, w_send, w_recv,
):
    tokens, width = x_ref.shape
    heads = codes_ref.shape[0]
    dim = width // heads
    rows, state = b_hbm.shape
    subs = tokens // SUB
    half = width // 2
    parts = len(cuts)
    seq = lax.axis_index("seq")
    z = lax.axis_index("head")
    chip = seq // 2
    core = seq % 2
    other = 1 - core
    sib = {"seq": chip * 2 + other, "head": z}

    def z_peer(d):
        return {"seq": seq, "head": (z + d) % zs}

    def chip_peer(d):
        return {"seq": ((chip + d) % chips) * 2 + core, "head": z}

    def copy(src, dst, send, recv, to):
        return pltpu.make_async_remote_copy(
            src_ref=src, dst_ref=dst, send_sem=send, recv_sem=recv,
            device_id=to, device_id_type=MESH,
        )

    loads = [
        pltpu.make_async_copy(src, dst, l_sem.at[i])
        for i, (src, dst) in enumerate([
            (codes_hbm, codes_ref), (rate_hbm, rate_ref), (gain_hbm, gain_ref),
            (b_hbm, bc.at[z, 0]), (c_hbm, bc.at[z, 1]), (g_hbm, g_ref), (x_hbm, x_ref),
        ])
    ]
    for each in loads:
        each.start()
    barrier = pltpu.get_barrier_semaphore()
    for d in range(1, zs):
        pl.semaphore_signal(barrier, inc=1, device_id=z_peer(d), device_id_type=MESH)
    for d in range(1, chips):
        pl.semaphore_signal(barrier, inc=1, device_id=chip_peer(d), device_id_type=MESH)
    pl.semaphore_signal(barrier, inc=1, device_id=sib, device_id_type=MESH)
    for each in loads[:3]:
        each.wait()

    eye = lax.broadcasted_iota(jnp.int32, (heads, heads), 0) == lax.broadcasted_iota(
        jnp.int32, (heads, heads), 1
    )
    rate = jnp.sum(jnp.where(eye, rate_ref[...], 0.0), axis=1, keepdims=True)
    gain = jnp.sum(jnp.where(eye, gain_ref[...], 0.0), axis=1, keepdims=True)
    codes = codes_ref[...]
    step = 0.5 + (codes & 1023).astype(F32) * (1.0 / 1024.0)
    log_decay = -rate * step - 0.1 * (codes >> 10).astype(F32)
    at_u = lax.broadcasted_iota(jnp.int32, (tokens, tokens), 0)
    at_t = lax.broadcasted_iota(jnp.int32, (tokens, tokens), 1)
    centred = jnp.where(
        at_u // SUB == at_t // SUB, jnp.where(at_u <= at_t, 0.5, -0.5), 0.0
    ).astype(BF16)
    logs = dot(split3(log_decay).astype(BF16), centred)
    logs = logs[:heads] + logs[heads : 2 * heads] + logs[2 * heads :]
    u3 = split3(jnp.exp(logs)).T.astype(BF16)
    v3 = split3(jnp.exp(-logs) * step).T.astype(BF16)
    lane = lax.broadcasted_iota(jnp.int32, (heads, width), 1)
    first = lax.broadcasted_iota(jnp.int32, (heads, width), 0) * dim
    own = (lane >= first) & (lane < first + dim)
    gain_s[...] = jnp.sum(jnp.where(own, gain, 0.0), axis=0, keepdims=True)
    ends = [
        jnp.exp(jnp.sum(log_decay, axis=1, keepdims=True)),
        jnp.exp(logs[:, SUB - 1 : SUB]),
        jnp.exp(logs[:, tokens - 1 :]),
    ]
    for i, end in enumerate(ends):
        end = jnp.sum(jnp.where(own, end, 0.0), axis=0, keepdims=True)
        dd[0, i] = end[:, :half]
        dd[1, i] = end[:, half:]
    spread_s[...] = jnp.concatenate([own.astype(F32)] * 3, axis=0).astype(BF16)
    for each in loads[3:5]:
        each.wait()
    pl.semaphore_wait(barrier, zs + chips - 1)
    gathers = [
        copy(bc.at[z], bc.at[z], g_send.at[d - 1], g_recv.at[d - 1], z_peer(d))
        for d in range(1, zs)
    ]
    for each in gathers:
        each.start()

    to_sib = copy(dd.at[other], dc.at[core], d_send.at[0], d_recv.at[0], sib)
    to_sib.start()
    dc[core] = dd[core]
    for each in loads[5:]:
        each.wait()

    def block(a):
        return slice(a * SUB, (a + 1) * SUB)

    def chunk(h, k):
        return slice(h * half + cuts[k][0], h * half + cuts[k][1])

    def root(a, lanes):
        return u_s[(a + 1) * SUB - 1 : (a + 1) * SUB, lanes]

    def factors(k):
        for h in range(2):
            lanes = chunk(h, k)
            u = dot(u3, spread_s[:, lanes])
            vs = dot(v3, spread_s[:, lanes])
            u_s[:, lanes] = u
            vs_s[:, lanes] = vs
            ug_s[:, lanes] = (u * g_ref[:, lanes].astype(F32)).astype(BF16)
            vx_s[:, lanes] = (vs * x_ref[:, lanes].astype(F32)).astype(BF16)

    for k in range(parts):
        factors(k)
    for each in gathers:
        each.wait()
    b_all = bc[:, 0].reshape(tokens, state)
    c_all = bc[:, 1].reshape(tokens, state)
    b_flip = b_all.astype(F32).T.astype(BF16)
    c_flip = c_all.astype(F32).T.astype(BF16)

    sib_copies = [
        copy(pa.at[other, :, :, chunk(0, k)], pc.at[core, :, :, chunk(0, k)], s_send.at[k], s_recv.at[k], sib)
        for k in range(parts)
    ]

    def summarize(k):
        for h in range(2):
            lanes = chunk(h, k)
            total = None
            for a in range(subs):
                r = root(a, lanes)
                ps = r * dot(b_flip[:, block(a)], vx_s[block(a), lanes])
                ad = r * dot(c_flip[:, block(a)], ug_s[block(a), lanes])
                ps_s[a, :, lanes] = ps
                as_s[a, :, lanes] = ad
                if a == 0:
                    p_dev, a_dev, total = ps, ad, r * r
                else:
                    p_dev = (r * r) * p_dev + ps
                    a_dev = a_dev + total * ad
                    total = total * (r * r)
            pa[h, 0, :, chunk(0, k)] = p_dev
            pa[h, 1, :, chunk(0, k)] = a_dev
        sib_copies[k].start()
        pc[core, :, :, chunk(0, k)] = pa[core, :, :, chunk(0, k)]

    to_chips = {}

    def combine(k):
        here = chunk(0, k)
        if k == 0:
            to_sib.wait()
            qt[...] = dc[0, 0] * dc[1, 0]
            for d in range(1, chips):
                each = copy(qt, rt.at[d - 1], t_send.at[d - 1], t_recv.at[d - 1], chip_peer(d))
                each.start()
                to_chips[d] = each
        sib_copies[k].wait()
        qb[0, :, here] = (dc[1, 0, :, here] * pc[0, 0, :, here] + pc[1, 0, :, here]).astype(BF16)
        qb[1, :, here] = (pc[0, 1, :, here] + dc[0, 0, :, here] * pc[1, 1, :, here]).astype(BF16)
        for d in range(1, chips):
            each = copy(
                qb.at[(chip + d) // chips, :, here], rq.at[d - 1, :, here],
                q_send.at[k, d - 1], q_recv.at[k, d - 1], chip_peer(d),
            )
            each.start()
            to_chips[k, d] = each

    summarize(0)
    for k in range(1, parts):
        summarize(k)
        combine(k - 1)
    combine(parts - 1)

    at_r = lax.broadcasted_iota(jnp.int32, (SUB, SUB), 0)
    at_c = lax.broadcasted_iota(jnp.int32, (SUB, SUB), 1)
    b_sums, c_sums = [], []
    for a in range(subs):
        b_a, c_a = b_all[block(a)], c_all[block(a)]
        scores = jnp.where(at_r >= at_c, dot(c_a, b_a, ((1,), (1,))), 0.0).astype(BF16)
        flipped = jnp.where(at_r <= at_c, dot(b_a, c_a, ((1,), (1,))), 0.0).astype(BF16)
        od_s[block(a)] = dot(scores, vx_s[block(a)])
        gd_s[block(a)] = dot(flipped, ug_s[block(a)])
        paired = dot(ug_s[block(a)], vx_s[block(a)], ((1,), (1,)))
        paired = jnp.where(at_r >= at_c, paired, 0.0)
        b_sums.append(split_dot(paired.T, c_a))
        c_sums.append(split_dot(paired, b_a))

    back = [
        copy(tmp.at[other, :, :, chunk(0, k)], ef.at[core, :, :, chunk(0, k)], e_send.at[k], e_recv.at[k], sib)
        for k in range(parts)
    ]

    def enter(k):
        here = chunk(0, k)
        for d in range(1, chips):
            if k == 0:
                to_chips[d].wait()
            to_chips[k, d].wait()
        size = cuts[k][1] - cuts[k][0]
        e_in = jnp.zeros((state, size), F32)
        f_in = jnp.zeros((state, size), F32)
        reach = jnp.ones((1, size), F32)
        for d in range(1, chips):
            e_in = e_in + jnp.where(chip >= d, reach, 0.0) * rq[d - 1, :, here].astype(F32)
            reach = reach * rt[d - 1, :, here]
        reach = jnp.ones((1, size), F32)
        for d in range(chips - 1, 0, -1):
            f_in = f_in + jnp.where(chip < d, reach, 0.0) * rq[d - 1, :, here].astype(F32)
            reach = reach * rt[d - 1, :, here]
        e_out = dc[0, 0, :, here] * e_in + pc[0, 0, :, here]
        f_out = dc[1, 0, :, here] * f_in + pc[1, 1, :, here]
        tmp[0, 0, :, here] = (dc[0, 1, :, here] * e_in).astype(BF16)
        tmp[1, 0, :, here] = (dc[1, 1, :, here] * e_out).astype(BF16)
        tmp[1, 1, :, here] = (dc[1, 2, :, here] * f_in).astype(BF16)
        tmp[0, 1, :, here] = (dc[0, 2, :, here] * f_out).astype(BF16)
        back[k].start()
        ef[core, :, :, here] = tmp[core, :, :, here]

    def states(k):
        back[k].wait()
        es = {}
        for h in range(2):
            lanes = chunk(h, k)
            es[h, 0, 0] = ef[h, 0, :, chunk(0, k)]
            es[h, subs - 1, 1] = ef[h, 1, :, chunk(0, k)]
            e = ef[h, 0, :, chunk(0, k)].astype(F32)
            for a in range(1, subs):
                r = root(a, lanes)
                e = r * (root(a - 1, lanes) * e + ps_s[a - 1, :, lanes])
                es[h, a, 0] = e.astype(BF16)
            f = ef[h, 1, :, chunk(0, k)].astype(F32)
            for a in range(subs - 2, -1, -1):
                r = root(a, lanes)
                f = r * (root(a + 1, lanes) * f + as_s[a + 1, :, lanes])
                es[h, a, 1] = f.astype(BF16)
            for a in range(subs):
                b_sums[a] += dot(vx_s[block(a), lanes], es[h, a, 1], ((1,), (1,)))
                c_sums[a] += dot(ug_s[block(a), lanes], es[h, a, 0], ((1,), (1,)))
        return es

    def outputs(k, es):
        for h in range(2):
            lanes = chunk(h, k)
            for a in range(subs):
                out = od_s[block(a), lanes] + dot(c_all[block(a)], es[h, a, 0])
                out = u_s[block(a), lanes] * out
                out = out + gain_s[:, lanes] * x_ref[block(a), lanes].astype(F32)
                out_ref[block(a), lanes] = out.astype(BF16)
                grad = gd_s[block(a), lanes] + dot(b_all[block(a)], es[h, a, 1])
                grad = vs_s[block(a), lanes] * grad
                grad = grad + gain_s[:, lanes] * g_ref[block(a), lanes].astype(F32)
                ig_ref[block(a), lanes] = grad.astype(BF16)

    def scatter(src, dst, send, recv):
        copies = [
            copy(src.at[(z + d) % zs], dst.at[d - 1], send.at[d - 1], recv.at[d - 1], z_peer(d))
            for d in range(1, zs)
        ]
        for each in copies:
            each.start()
        return copies

    def scatter_early():
        part[:, 0] = jnp.concatenate(b_sums, axis=0).reshape(zs, rows, state)
        part[:, 1] = jnp.concatenate(c_sums, axis=0).reshape(zs, rows, state)
        for a in range(subs):
            b_sums[a] = jnp.zeros((SUB, state), F32)
            c_sums[a] = jnp.zeros((SUB, state), F32)
        return scatter(part, rpart, r_send, r_recv)

    early = parts - 4
    held = []
    if early < 0:
        sent = scatter_early()
    enter(0)
    for k in range(1, parts):
        enter(k)
        es = states(k - 1)
        if k - 1 == early:
            sent = scatter_early()
        if k - 1 <= early:
            outputs(k - 1, es)
        else:
            held.append((k - 1, es))
    held.append((parts - 1, states(parts - 1)))
    late[:, 0] = jnp.concatenate(b_sums, axis=0).reshape(zs, rows, state)
    late[:, 1] = jnp.concatenate(c_sums, axis=0).reshape(zs, rows, state)
    lpart[...] = late[...].astype(BF16)
    sent_late = scatter(lpart, rlate, w_send, w_recv)
    for k, es in held:
        outputs(k, es)
    gb = part[z, 0] + late[z, 0]
    gc = part[z, 1] + late[z, 1]
    for d in range(zs - 1):
        sent[d].wait()
        gb = gb + rpart[d, 0]
        gc = gc + rpart[d, 1]
    for d in range(zs - 1):
        sent_late[d].wait()
        gb = gb + rlate[d, 0].astype(F32)
        gc = gc + rlate[d, 1].astype(F32)
    gb_ref[...] = gb
    gc_ref[...] = gc


def chunks(half):
    units = half // 128
    sizes = [1] * units
    if units >= 4:
        sizes = [1] + [2] * ((units - 2) // 2) + [1] * (1 + units % 2)
    cuts, at = [], 0
    for size in sizes:
        cuts.append((at, at + 128 * size))
        at += 128 * size
    return cuts


def hand_over(*refs):
    count = (len(refs) - 1) // 2
    sems = refs[-1]
    copies = []
    for i in range(count):
        src, dst = refs[i], refs[count + i]
        rows = src.shape[0] // 4
        for j in range(4):
            here = pl.ds(j * rows, rows)
            copies.append(pltpu.make_async_copy(src.at[here], dst.at[here], sems.at[i, j]))
    for each in copies:
        each.start()
    for each in copies:
        each.wait()


def local(x_in, b_in, c_in, decay_codes, decay_rate, skip_gain, out_grad):
    tokens, width = x_in.shape
    rows, state = b_in.shape
    heads = decay_codes.shape[0]
    subs = tokens // SUB
    half = width // 2
    cuts = chunks(half)
    parts = len(cuts)
    chips = lax.axis_size("seq") // 2
    zs = lax.axis_size("head")
    vmem = pl.BlockSpec(memory_space=pltpu.VMEM)
    hbm = pl.BlockSpec(memory_space=pltpu.MemorySpace.HBM)
    dma = pltpu.SemaphoreType.DMA
    results = pl.pallas_call(
        functools.partial(kernel, chips, zs, cuts),
        out_shape=(
            pltpu.MemorySpace.VMEM((tokens, width), BF16),
            pltpu.MemorySpace.VMEM((tokens, width), BF16),
            pltpu.MemorySpace.VMEM((rows, state), F32),
            pltpu.MemorySpace.VMEM((rows, state), F32),
        ),
        in_specs=[hbm] * 7,
        out_specs=(vmem,) * 4,
        scratch_shapes=[
            pltpu.VMEM((tokens, width), BF16),
            pltpu.VMEM((tokens, width), BF16),
            pltpu.VMEM(decay_codes.shape, jnp.int32),
            pltpu.VMEM((1, heads), F32),
            pltpu.VMEM((1, heads), F32),
            pltpu.VMEM((tokens, width), F32),
            pltpu.VMEM((tokens, width), F32),
            pltpu.VMEM((tokens, width), BF16),
            pltpu.VMEM((tokens, width), BF16),
            pltpu.VMEM((tokens, width), F32),
            pltpu.VMEM((tokens, width), F32),
            pltpu.VMEM((subs, state, width), F32),
            pltpu.VMEM((subs, state, width), F32),
            pltpu.VMEM((1, width), F32),
            pltpu.VMEM((3 * heads, width), BF16),
            pltpu.VMEM((zs, 2, rows, state), BF16),
            pltpu.VMEM((2, 2, state, half), F32),
            pltpu.VMEM((2, 3, 1, half), F32),
            pltpu.VMEM((2, 2, state, half), F32),
            pltpu.VMEM((2, 3, 1, half), F32),
            pltpu.VMEM((2, state, half), BF16),
            pltpu.VMEM((1, half), F32),
            pltpu.VMEM((chips - 1, state, half), BF16),
            pltpu.VMEM((chips - 1, 1, half), F32),
            pltpu.VMEM((2, 2, state, half), BF16),
            pltpu.VMEM((2, 2, state, half), BF16),
            pltpu.VMEM((zs, 2, rows, state), F32),
            pltpu.VMEM((zs - 1, 2, rows, state), F32),
            pltpu.VMEM((zs, 2, rows, state), F32),
            pltpu.VMEM((zs, 2, rows, state), BF16),
            pltpu.VMEM((zs - 1, 2, rows, state), BF16),
            dma((7,)),
            dma((zs - 1,)), dma((zs - 1,)),
            dma((1,)), dma((1,)),
            dma((parts,)), dma((parts,)),
            dma((parts,)), dma((parts,)),
            dma((parts, chips - 1)), dma((parts, chips - 1)),
            dma((chips - 1,)), dma((chips - 1,)),
            dma((zs - 1,)), dma((zs - 1,)),
            dma((zs - 1,)), dma((zs - 1,)),
        ],
        compiler_params=pltpu.CompilerParams(
            collective_id=0, has_side_effects=True, vmem_limit_bytes=58 * 1024 * 1024
        ),
    )(
        x_in, b_in, c_in, decay_codes,
        decay_rate.reshape(1, heads), skip_gain.reshape(1, heads), out_grad,
    )
    return pl.pallas_call(
        hand_over,
        out_shape=tuple(jax.ShapeDtypeStruct(r.shape, r.dtype) for r in results),
        in_specs=[vmem] * 4,
        out_specs=(hbm,) * 4,
        scratch_shapes=[dma((4, 4))],
        compiler_params=pltpu.CompilerParams(vmem_limit_bytes=4 * 1024 * 1024),
    )(*results)


def solution(mesh):
    placed = (
        P("seq", "head"),
        P(("seq", "head"), None),
        P(("seq", "head"), None),
        P("head", "seq"),
        P("head"),
        P("head"),
        P("seq", "head"),
    )
    return jax.shard_map(
        local,
        mesh=mesh,
        in_specs=placed,
        out_specs=(
            P("seq", "head"),
            P("seq", "head"),
            P(("seq", "head"), None),
            P(("seq", "head"), None),
        ),
        check_vma=False,
    )
```

```python
import functools

import jax
import jax.numpy as jnp
from jax import lax
from jax.experimental import pallas as pl
from jax.experimental.pallas import tpu as pltpu
from jax.sharding import PartitionSpec as P

SUB = 128
MESH = pl.DeviceIdType.MESH
F32 = jnp.float32
BF16 = jnp.bfloat16


def dot(a, b, dims=((1,), (0,))):
    return lax.dot_general(a, b, (dims, ((), ())), preferred_element_type=F32)


def split3(a):
    hi = a.astype(BF16).astype(F32)
    mid = (a - hi).astype(BF16).astype(F32)
    low = a - hi - mid
    return jnp.concatenate([hi, mid, low], axis=0)


def split_dot(a, b, dims=((1,), (0,))):
    hi = a.astype(BF16)
    low = (a - hi.astype(F32)).astype(BF16)
    return dot(hi, b, dims) + dot(low, b, dims)


def kernel(
    chips, zs, cuts,
    x_hbm, b_hbm, c_hbm, codes_hbm, rate_hbm, gain_hbm, g_hbm,
    out_ref, ig_ref, gb_ref, gc_ref,
    x_ref, g_ref, codes_ref, rate_ref, gain_ref,
    u_s, vs_s, ug_s, vx_s, od_s, gd_s, ps_s, as_s, gain_s, spread_s,
    bc, pa, dd, pc, dc, qb, qt, rq, rt, tmp, ef, part, rpart, late, lpart, rlate,
    l_sem, g_send, g_recv, d_send, d_recv, s_send, s_recv, e_send, e_recv,
    q_send, q_recv, t_send, t_recv, r_send, r_recv, w_send, w_recv,
):
    tokens, width = x_ref.shape
    heads = codes_ref.shape[0]
    dim = width // heads
    rows, state = b_hbm.shape
    subs = tokens // SUB
    half = width // 2
    parts = len(cuts)
    seq = lax.axis_index("seq")
    z = lax.axis_index("head")
    chip = seq // 2
    core = seq % 2
    other = 1 - core
    sib = {"seq": chip * 2 + other, "head": z}

    def z_peer(d):
        return {"seq": seq, "head": (z + d) % zs}

    def chip_peer(d):
        return {"seq": ((chip + d) % chips) * 2 + core, "head": z}

    def copy(src, dst, send, recv, to):
        return pltpu.make_async_remote_copy(
            src_ref=src, dst_ref=dst, send_sem=send, recv_sem=recv,
            device_id=to, device_id_type=MESH,
        )

    loads = [
        pltpu.make_async_copy(src, dst, l_sem.at[i])
        for i, (src, dst) in enumerate([
            (codes_hbm, codes_ref), (rate_hbm, rate_ref), (gain_hbm, gain_ref),
            (b_hbm, bc.at[z, 0]), (c_hbm, bc.at[z, 1]), (g_hbm, g_ref), (x_hbm, x_ref),
        ])
    ]
    for each in loads:
        each.start()
    barrier = pltpu.get_barrier_semaphore()
    for d in range(1, zs):
        pl.semaphore_signal(barrier, inc=1, device_id=z_peer(d), device_id_type=MESH)
    for d in range(1, chips):
        pl.semaphore_signal(barrier, inc=1, device_id=chip_peer(d), device_id_type=MESH)
    pl.semaphore_signal(barrier, inc=1, device_id=sib, device_id_type=MESH)
    for each in loads[:3]:
        each.wait()

    eye = lax.broadcasted_iota(jnp.int32, (heads, heads), 0) == lax.broadcasted_iota(
        jnp.int32, (heads, heads), 1
    )
    rate = jnp.sum(jnp.where(eye, rate_ref[...], 0.0), axis=1, keepdims=True)
    gain = jnp.sum(jnp.where(eye, gain_ref[...], 0.0), axis=1, keepdims=True)
    codes = codes_ref[...]
    step = 0.5 + (codes & 1023).astype(F32) * (1.0 / 1024.0)
    log_decay = -rate * step - 0.1 * (codes >> 10).astype(F32)
    at_u = lax.broadcasted_iota(jnp.int32, (tokens, tokens), 0)
    at_t = lax.broadcasted_iota(jnp.int32, (tokens, tokens), 1)
    centred = jnp.where(
        at_u // SUB == at_t // SUB, jnp.where(at_u <= at_t, 0.5, -0.5), 0.0
    ).astype(BF16)
    logs = dot(split3(log_decay).astype(BF16), centred)
    logs = logs[:heads] + logs[heads : 2 * heads] + logs[2 * heads :]
    u3 = split3(jnp.exp(logs)).T.astype(BF16)
    v3 = split3(jnp.exp(-logs) * step).T.astype(BF16)
    lane = lax.broadcasted_iota(jnp.int32, (heads, width), 1)
    first = lax.broadcasted_iota(jnp.int32, (heads, width), 0) * dim
    own = (lane >= first) & (lane < first + dim)
    gain_s[...] = jnp.sum(jnp.where(own, gain, 0.0), axis=0, keepdims=True)
    ends = [
        jnp.exp(jnp.sum(log_decay, axis=1, keepdims=True)),
        jnp.exp(logs[:, SUB - 1 : SUB]),
        jnp.exp(logs[:, tokens - 1 :]),
    ]
    for i, end in enumerate(ends):
        end = jnp.sum(jnp.where(own, end, 0.0), axis=0, keepdims=True)
        dd[0, i] = end[:, :half]
        dd[1, i] = end[:, half:]
    spread_s[...] = jnp.concatenate([own.astype(F32)] * 3, axis=0).astype(BF16)
    for each in loads[3:5]:
        each.wait()
    pl.semaphore_wait(barrier, zs + chips - 1)
    gathers = [
        copy(bc.at[z], bc.at[z], g_send.at[d - 1], g_recv.at[d - 1], z_peer(d))
        for d in range(1, zs)
    ]
    for each in gathers:
        each.start()

    to_sib = copy(dd.at[other], dc.at[core], d_send.at[0], d_recv.at[0], sib)
    to_sib.start()
    dc[core] = dd[core]
    for each in loads[5:]:
        each.wait()

    def block(a):
        return slice(a * SUB, (a + 1) * SUB)

    def chunk(h, k):
        return slice(h * half + cuts[k][0], h * half + cuts[k][1])

    def root(a, lanes):
        return u_s[(a + 1) * SUB - 1 : (a + 1) * SUB, lanes]

    def factors(k):
        for h in range(2):
            lanes = chunk(h, k)
            u = dot(u3, spread_s[:, lanes])
            vs = dot(v3, spread_s[:, lanes])
            u_s[:, lanes] = u
            vs_s[:, lanes] = vs
            ug_s[:, lanes] = (u * g_ref[:, lanes].astype(F32)).astype(BF16)
            vx_s[:, lanes] = (vs * x_ref[:, lanes].astype(F32)).astype(BF16)

    for k in range(parts):
        factors(k)
    for each in gathers:
        each.wait()
    b_all = bc[:, 0].reshape(tokens, state)
    c_all = bc[:, 1].reshape(tokens, state)
    b_flip = b_all.astype(F32).T.astype(BF16)
    c_flip = c_all.astype(F32).T.astype(BF16)

    sib_copies = [
        copy(pa.at[other, :, :, chunk(0, k)], pc.at[core, :, :, chunk(0, k)], s_send.at[k], s_recv.at[k], sib)
        for k in range(parts)
    ]

    def summarize(k):
        for h in range(2):
            lanes = chunk(h, k)
            total = None
            for a in range(subs):
                r = root(a, lanes)
                ps = r * dot(b_flip[:, block(a)], vx_s[block(a), lanes])
                ad = r * dot(c_flip[:, block(a)], ug_s[block(a), lanes])
                ps_s[a, :, lanes] = ps
                as_s[a, :, lanes] = ad
                if a == 0:
                    p_dev, a_dev, total = ps, ad, r * r
                else:
                    p_dev = (r * r) * p_dev + ps
                    a_dev = a_dev + total * ad
                    total = total * (r * r)
            pa[h, 0, :, chunk(0, k)] = p_dev
            pa[h, 1, :, chunk(0, k)] = a_dev
        sib_copies[k].start()
        pc[core, :, :, chunk(0, k)] = pa[core, :, :, chunk(0, k)]

    to_chips = {}

    def combine(k):
        here = chunk(0, k)
        if k == 0:
            to_sib.wait()
            qt[...] = dc[0, 0] * dc[1, 0]
            for d in range(1, chips):
                each = copy(qt, rt.at[d - 1], t_send.at[d - 1], t_recv.at[d - 1], chip_peer(d))
                each.start()
                to_chips[d] = each
        sib_copies[k].wait()
        qb[0, :, here] = (dc[1, 0, :, here] * pc[0, 0, :, here] + pc[1, 0, :, here]).astype(BF16)
        qb[1, :, here] = (pc[0, 1, :, here] + dc[0, 0, :, here] * pc[1, 1, :, here]).astype(BF16)
        for d in range(1, chips):
            each = copy(
                qb.at[(chip + d) // chips, :, here], rq.at[d - 1, :, here],
                q_send.at[k, d - 1], q_recv.at[k, d - 1], chip_peer(d),
            )
            each.start()
            to_chips[k, d] = each

    summarize(0)
    for k in range(1, parts):
        summarize(k)
        combine(k - 1)
    combine(parts - 1)

    at_r = lax.broadcasted_iota(jnp.int32, (SUB, SUB), 0)
    at_c = lax.broadcasted_iota(jnp.int32, (SUB, SUB), 1)
    b_sums, c_sums = [], []
    for a in range(subs):
        b_a, c_a = b_all[block(a)], c_all[block(a)]
        scores = jnp.where(at_r >= at_c, dot(c_a, b_a, ((1,), (1,))), 0.0).astype(BF16)
        flipped = jnp.where(at_r <= at_c, dot(b_a, c_a, ((1,), (1,))), 0.0).astype(BF16)
        od_s[block(a)] = dot(scores, vx_s[block(a)])
        gd_s[block(a)] = dot(flipped, ug_s[block(a)])
        paired = dot(ug_s[block(a)], vx_s[block(a)], ((1,), (1,)))
        paired = jnp.where(at_r >= at_c, paired, 0.0)
        b_sums.append(split_dot(paired.T, c_a))
        c_sums.append(split_dot(paired, b_a))

    back = [
        copy(tmp.at[other, :, :, chunk(0, k)], ef.at[core, :, :, chunk(0, k)], e_send.at[k], e_recv.at[k], sib)
        for k in range(parts)
    ]

    def enter(k):
        here = chunk(0, k)
        for d in range(1, chips):
            if k == 0:
                to_chips[d].wait()
            to_chips[k, d].wait()
        size = cuts[k][1] - cuts[k][0]
        e_in = jnp.zeros((state, size), F32)
        f_in = jnp.zeros((state, size), F32)
        reach = jnp.ones((1, size), F32)
        for d in range(1, chips):
            e_in = e_in + jnp.where(chip >= d, reach, 0.0) * rq[d - 1, :, here].astype(F32)
            reach = reach * rt[d - 1, :, here]
        reach = jnp.ones((1, size), F32)
        for d in range(chips - 1, 0, -1):
            f_in = f_in + jnp.where(chip < d, reach, 0.0) * rq[d - 1, :, here].astype(F32)
            reach = reach * rt[d - 1, :, here]
        e_out = dc[0, 0, :, here] * e_in + pc[0, 0, :, here]
        f_out = dc[1, 0, :, here] * f_in + pc[1, 1, :, here]
        tmp[0, 0, :, here] = (dc[0, 1, :, here] * e_in).astype(BF16)
        tmp[1, 0, :, here] = (dc[1, 1, :, here] * e_out).astype(BF16)
        tmp[1, 1, :, here] = (dc[1, 2, :, here] * f_in).astype(BF16)
        tmp[0, 1, :, here] = (dc[0, 2, :, here] * f_out).astype(BF16)
        back[k].start()
        ef[core, :, :, here] = tmp[core, :, :, here]

    def states(k):
        back[k].wait()
        es = {}
        for h in range(2):
            lanes = chunk(h, k)
            es[h, 0, 0] = ef[h, 0, :, chunk(0, k)]
            es[h, subs - 1, 1] = ef[h, 1, :, chunk(0, k)]
            e = ef[h, 0, :, chunk(0, k)].astype(F32)
            for a in range(1, subs):
                r = root(a, lanes)
                e = r * (root(a - 1, lanes) * e + ps_s[a - 1, :, lanes])
                es[h, a, 0] = e.astype(BF16)
            f = ef[h, 1, :, chunk(0, k)].astype(F32)
            for a in range(subs - 2, -1, -1):
                r = root(a, lanes)
                f = r * (root(a + 1, lanes) * f + as_s[a + 1, :, lanes])
                es[h, a, 1] = f.astype(BF16)
            for a in range(subs):
                b_sums[a] += dot(vx_s[block(a), lanes], es[h, a, 1], ((1,), (1,)))
                c_sums[a] += dot(ug_s[block(a), lanes], es[h, a, 0], ((1,), (1,)))
        return es

    def outputs(k, es):
        for h in range(2):
            lanes = chunk(h, k)
            for a in range(subs):
                out = od_s[block(a), lanes] + dot(c_all[block(a)], es[h, a, 0])
                out = u_s[block(a), lanes] * out
                out = out + gain_s[:, lanes] * x_ref[block(a), lanes].astype(F32)
                out_ref[block(a), lanes] = out.astype(BF16)
                grad = gd_s[block(a), lanes] + dot(b_all[block(a)], es[h, a, 1])
                grad = vs_s[block(a), lanes] * grad
                grad = grad + gain_s[:, lanes] * g_ref[block(a), lanes].astype(F32)
                ig_ref[block(a), lanes] = grad.astype(BF16)

    def scatter(src, dst, send, recv):
        copies = [
            copy(src.at[(z + d) % zs], dst.at[d - 1], send.at[d - 1], recv.at[d - 1], z_peer(d))
            for d in range(1, zs)
        ]
        for each in copies:
            each.start()
        return copies

    def scatter_early():
        part[:, 0] = jnp.concatenate(b_sums, axis=0).reshape(zs, rows, state)
        part[:, 1] = jnp.concatenate(c_sums, axis=0).reshape(zs, rows, state)
        for a in range(subs):
            b_sums[a] = jnp.zeros((SUB, state), F32)
            c_sums[a] = jnp.zeros((SUB, state), F32)
        return scatter(part, rpart, r_send, r_recv)

    early = parts - 4
    held = []
    if early < 0:
        sent = scatter_early()
    enter(0)
    for k in range(1, parts):
        enter(k)
        es = states(k - 1)
        if k - 1 == early:
            sent = scatter_early()
        if k - 1 <= early:
            outputs(k - 1, es)
        else:
            held.append((k - 1, es))
    held.append((parts - 1, states(parts - 1)))
    late[:, 0] = jnp.concatenate(b_sums, axis=0).reshape(zs, rows, state)
    late[:, 1] = jnp.concatenate(c_sums, axis=0).reshape(zs, rows, state)
    lpart[...] = late[...].astype(BF16)
    sent_late = scatter(lpart, rlate, w_send, w_recv)
    for k, es in held:
        outputs(k, es)
    gb = part[z, 0] + late[z, 0]
    gc = part[z, 1] + late[z, 1]
    for d in range(zs - 1):
        sent[d].wait()
        gb = gb + rpart[d, 0]
        gc = gc + rpart[d, 1]
    for d in range(zs - 1):
        sent_late[d].wait()
        gb = gb + rlate[d, 0].astype(F32)
        gc = gc + rlate[d, 1].astype(F32)
    gb_ref[...] = gb
    gc_ref[...] = gc


def chunks(half):
    units = half // 128
    sizes = [1] * units
    if units >= 6:
        sizes = [1, 1] + [2] * ((units - 4) // 2) + [1] * (2 + units % 2)
    cuts, at = [], 0
    for size in sizes:
        cuts.append((at, at + 128 * size))
        at += 128 * size
    return cuts


def hand_over(*refs):
    count = (len(refs) - 1) // 2
    sems = refs[-1]
    copies = []
    for i in range(count):
        src, dst = refs[i], refs[count + i]
        rows = src.shape[0] // 4
        for j in range(4):
            here = pl.ds(j * rows, rows)
            copies.append(pltpu.make_async_copy(src.at[here], dst.at[here], sems.at[i, j]))
    for each in copies:
        each.start()
    for each in copies:
        each.wait()


def local(x_in, b_in, c_in, decay_codes, decay_rate, skip_gain, out_grad):
    tokens, width = x_in.shape
    rows, state = b_in.shape
    heads = decay_codes.shape[0]
    subs = tokens // SUB
    half = width // 2
    cuts = chunks(half)
    parts = len(cuts)
    chips = lax.axis_size("seq") // 2
    zs = lax.axis_size("head")
    vmem = pl.BlockSpec(memory_space=pltpu.VMEM)
    hbm = pl.BlockSpec(memory_space=pltpu.MemorySpace.HBM)
    dma = pltpu.SemaphoreType.DMA
    results = pl.pallas_call(
        functools.partial(kernel, chips, zs, cuts),
        out_shape=(
            pltpu.MemorySpace.VMEM((tokens, width), BF16),
            pltpu.MemorySpace.VMEM((tokens, width), BF16),
            pltpu.MemorySpace.VMEM((rows, state), F32),
            pltpu.MemorySpace.VMEM((rows, state), F32),
        ),
        in_specs=[hbm] * 7,
        out_specs=(vmem,) * 4,
        scratch_shapes=[
            pltpu.VMEM((tokens, width), BF16),
            pltpu.VMEM((tokens, width), BF16),
            pltpu.VMEM(decay_codes.shape, jnp.int32),
            pltpu.VMEM((1, heads), F32),
            pltpu.VMEM((1, heads), F32),
            pltpu.VMEM((tokens, width), F32),
            pltpu.VMEM((tokens, width), F32),
            pltpu.VMEM((tokens, width), BF16),
            pltpu.VMEM((tokens, width), BF16),
            pltpu.VMEM((tokens, width), F32),
            pltpu.VMEM((tokens, width), F32),
            pltpu.VMEM((subs, state, width), F32),
            pltpu.VMEM((subs, state, width), F32),
            pltpu.VMEM((1, width), F32),
            pltpu.VMEM((3 * heads, width), BF16),
            pltpu.VMEM((zs, 2, rows, state), BF16),
            pltpu.VMEM((2, 2, state, half), F32),
            pltpu.VMEM((2, 3, 1, half), F32),
            pltpu.VMEM((2, 2, state, half), F32),
            pltpu.VMEM((2, 3, 1, half), F32),
            pltpu.VMEM((2, state, half), BF16),
            pltpu.VMEM((1, half), F32),
            pltpu.VMEM((chips - 1, state, half), BF16),
            pltpu.VMEM((chips - 1, 1, half), F32),
            pltpu.VMEM((2, 2, state, half), BF16),
            pltpu.VMEM((2, 2, state, half), BF16),
            pltpu.VMEM((zs, 2, rows, state), F32),
            pltpu.VMEM((zs - 1, 2, rows, state), F32),
            pltpu.VMEM((zs, 2, rows, state), F32),
            pltpu.VMEM((zs, 2, rows, state), BF16),
            pltpu.VMEM((zs - 1, 2, rows, state), BF16),
            dma((7,)),
            dma((zs - 1,)), dma((zs - 1,)),
            dma((1,)), dma((1,)),
            dma((parts,)), dma((parts,)),
            dma((parts,)), dma((parts,)),
            dma((parts, chips - 1)), dma((parts, chips - 1)),
            dma((chips - 1,)), dma((chips - 1,)),
            dma((zs - 1,)), dma((zs - 1,)),
            dma((zs - 1,)), dma((zs - 1,)),
        ],
        compiler_params=pltpu.CompilerParams(
            collective_id=0, has_side_effects=True, vmem_limit_bytes=58 * 1024 * 1024
        ),
    )(
        x_in, b_in, c_in, decay_codes,
        decay_rate.reshape(1, heads), skip_gain.reshape(1, heads), out_grad,
    )
    return pl.pallas_call(
        hand_over,
        out_shape=tuple(jax.ShapeDtypeStruct(r.shape, r.dtype) for r in results),
        in_specs=[vmem] * 4,
        out_specs=(hbm,) * 4,
        scratch_shapes=[dma((4, 4))],
        compiler_params=pltpu.CompilerParams(vmem_limit_bytes=4 * 1024 * 1024),
    )(*results)


def solution(mesh):
    placed = (
        P("seq", "head"),
        P(("seq", "head"), None),
        P(("seq", "head"), None),
        P("head", "seq"),
        P("head"),
        P("head"),
        P("seq", "head"),
    )
    return jax.shard_map(
        local,
        mesh=mesh,
        in_specs=placed,
        out_specs=(
            P("seq", "head"),
            P("seq", "head"),
            P(("seq", "head"), None),
            P(("seq", "head"), None),
        ),
        check_vma=False,
    )
```
